256 devices in a mesh: pb: 16 (over z, y_lo), ka: 16 (over y_hi, x, core).
Axes of the slice: x: 4, y: 4 (y_hi: 2, y_lo: 2; y = y_hi * 2 + y_lo), z: 8, core: 2. Of those that a mesh axis runs over, the one named last changes fastest.
Arguments:
- queries: bfloat16 [65536, 768], P(('pb', 'ka')), may hold values from -5 to 5
- key_heads: bfloat16 [65536, 128], P(('pb', 'ka')), may hold values from -5 to 5
- value_heads: bfloat16 [65536, 128], P(('pb', 'ka')), may hold values from -6 to 6
- grad_output: bfloat16 [65536, 768], P(('pb', 'ka')), may hold values from -6 to 6
- token_logprob: float32 [65536], P(('pb', 'ka')), may hold values from -8 to -0.05
- doc_ids: int32 [65536], P(('pb', 'ka')), may hold values from 0 to 63, as said below
- response: int32 [65536], P(('pb', 'ka')), may hold values from 0 to 1, as said below
Outputs:
- attention: bfloat16 [65536, 768], P(('pb', 'ka'))
- grad_queries: float32 [65536, 768], P(('pb', 'ka'))
- grad_keys: float32 [65536, 128], P(('pb', 'ka'))
- grad_values: float32 [65536, 128], P(('pb', 'ka'))
- margins: float32 [32], replicated
The draws below stay inside these ranges and needn't reach their ends.
Inputs may be any that keep to these rules, and one draw needn't show every extreme that they name: `doc_ids`: never falling; documents 2p and 2p + 1 are the chosen and the rejected sequence of pair p and together fill positions p * 2048 to (p + 1) * 2048 - 1; every document starts at a multiple of 8 positions and has 8 positions or more; some document has exactly 2040 positions. Each document is 1 or more prompt positions followed by 1 or more response positions; both documents of a pair have prompts of equal length.
All inputs are finite; a program needn't handle non-finite values.
Results may differ from the reference program's by a relative error of at most 0.03.
Values may be sent and summed in bfloat16 or wider, within the bound.
No kernel may reach another device: no remote copies, remote signals or barrier semaphores. Data moves between devices by JAX's collectives and lax.ppermute only.
A program may use at most 64 MiB of HBM per device.

```python
import math
import jax
import jax.numpy as jnp
from jax import lax

HEAD_DIM = 128
GROUP_Q = 6
KV_GROUPS = 1
PAIR_SPAN = 2048
SEQ = 65536
HEADS = 6
PAIRS = 32


def doc_layout(key):
    span_units = PAIR_SPAN // 8
    chosen_units = jax.random.randint(key, (PAIRS,), 1, span_units).astype(jnp.int32)
    forced = jax.random.randint(jax.random.fold_in(key, 7), (), 0, PAIRS).astype(jnp.int32)
    edge_pick = jax.random.randint(jax.random.fold_in(key, 9), (), 0, 2).astype(jnp.int32)
    edge_units = jnp.where(edge_pick == 0, 1, span_units - 1).astype(jnp.int32)
    chosen_units = jnp.where(jnp.arange(PAIRS, dtype=jnp.int32) == forced, edge_units, chosen_units)
    chosen_len = (chosen_units * 8).astype(jnp.int32)
    pair_least = jnp.minimum(chosen_len, PAIR_SPAN - chosen_len)
    prompt = jax.random.randint(jax.random.fold_in(key, 5), (PAIRS,), 1, pair_least).astype(jnp.int32)
    position = jnp.arange(SEQ, dtype=jnp.int32)
    pair_of = position // PAIR_SPAN
    inside = position - pair_of * PAIR_SPAN
    second = (inside >= chosen_len[pair_of]).astype(jnp.int32)
    document = (2 * pair_of + second).astype(jnp.int32)
    doc_start = second * chosen_len[pair_of]
    answer = (inside - doc_start >= prompt[pair_of]).astype(jnp.int32)
    return (document, answer)


def draw_doc_ids(key, part):
    document, answer = doc_layout(key)
    return document


def draw_response(key, part):
    document, answer = doc_layout(key)
    return answer


def draw_queries(key, part):
    key = jax.random.fold_in(key, 11)
    values = jnp.clip(jax.random.normal(key, (SEQ, KV_GROUPS, GROUP_Q, HEAD_DIM), jnp.float32), -4.0, 4.0)
    return values.reshape(SEQ, KV_GROUPS * GROUP_Q * HEAD_DIM).astype(jnp.bfloat16)


def draw_key_heads(key, part):
    key = jax.random.fold_in(key, 23)
    values = jnp.clip(jax.random.normal(key, (SEQ, KV_GROUPS, HEAD_DIM), jnp.float32), -4.0, 4.0)
    return values.reshape(SEQ, KV_GROUPS * HEAD_DIM).astype(jnp.bfloat16)


def block_scale(key, shape, pieces, low, largest):
    gain, own = 1.0, jax.random.fold_in(key, 6)
    for dim, blocks in pieces:
        steps = jnp.exp(jax.random.uniform(jax.random.fold_in(own, dim), (blocks,), jnp.float32, low / len(pieces), largest / len(pieces)))
        gain = gain * jnp.repeat(steps, shape[dim] // blocks).reshape([-1 if axis == dim else 1 for axis in range(len(shape))])
    return gain


def centred(own_key, extent, scale, reach, split=(), held_as=jnp.bfloat16):
    gain = block_scale(own_key, extent, split, -0.22, 0.18) if split else 1.0
    values = jax.random.normal(own_key, extent, jnp.float32) * scale * gain
    return jnp.minimum(jnp.maximum(values, -reach), reach).astype(held_as)


def setup_inputs(seed: int = 0) -> dict:
    key_list = jax.random.split(jax.random.key(seed), 8)
    queries = draw_queries(jax.random.fold_in(key_list[7], 71), 0)
    key_heads = draw_key_heads(jax.random.fold_in(key_list[7], 71), 0)
    value_heads = centred(key_list[2], (SEQ, KV_GROUPS * HEAD_DIM), 1.0, 6.0, ((0, 256),))
    grad_output = centred(key_list[3], (SEQ, HEADS * HEAD_DIM), 1.0, 6.0, ((0, 256),))
    token_logprob = jnp.clip(-8.0 + 7.95 * jax.random.uniform(key_list[4], (SEQ,), jnp.float32) ** block_scale(key_list[4], (SEQ,), ((0, 256),), -0.2, 0.2), -8.0, -0.05)
    doc_ids = draw_doc_ids(jax.random.fold_in(key_list[7], 71), 0)
    response = draw_response(jax.random.fold_in(key_list[7], 71), 0)
    return dict(queries=queries, key_heads=key_heads, value_heads=value_heads, grad_output=grad_output, token_logprob=token_logprob, doc_ids=doc_ids, response=response)


NEG = -1e+30

def head_pass(query_head, grad_head, key_group, value_group, allowed):
    inv_root = 1.0 / math.sqrt(HEAD_DIM)
    scores = jnp.dot(query_head, key_group.T, preferred_element_type=jnp.float32) * inv_root
    scores = jnp.where(allowed, scores, NEG)
    row_max = lax.optimization_barrier(jnp.max(scores, axis=1))
    row_sum = lax.optimization_barrier(jnp.sum(jnp.where(allowed, jnp.exp(scores - row_max[:, None]), 0.0), axis=1))
    log_total = row_max + jnp.log(row_sum)
    probs = jnp.where(allowed, jnp.exp(scores - log_total[:, None]), 0.0).astype(jnp.bfloat16)
    output = jnp.dot(probs, value_group, preferred_element_type=jnp.float32).astype(jnp.bfloat16)
    delta = lax.optimization_barrier(jnp.sum(grad_head.astype(jnp.float32) * output.astype(jnp.float32), axis=1))
    grad_prob = jnp.dot(grad_head, value_group.T, preferred_element_type=jnp.float32)
    grad_score = (probs.astype(jnp.float32) * (grad_prob - delta[:, None])).astype(jnp.bfloat16)
    grad_query = jnp.dot(grad_score, key_group, preferred_element_type=jnp.float32) * inv_root
    grad_key = jnp.dot(grad_score.T, query_head, preferred_element_type=jnp.float32) * inv_root
    grad_value = jnp.dot(probs.T, grad_head, preferred_element_type=jnp.float32)
    return (output, grad_query, grad_key, grad_value)

def span_pass(queries, key_heads, value_heads, grad_output, doc_ids, number):
    start = (number * PAIR_SPAN).astype(jnp.int32)
    span_queries = lax.dynamic_slice_in_dim(queries, start, PAIR_SPAN, 0)
    span_keys = lax.dynamic_slice_in_dim(key_heads, start, PAIR_SPAN, 0)
    span_values = lax.dynamic_slice_in_dim(value_heads, start, PAIR_SPAN, 0)
    span_grads = lax.dynamic_slice_in_dim(grad_output, start, PAIR_SPAN, 0)
    span_docs = lax.dynamic_slice_in_dim(doc_ids, start, PAIR_SPAN, 0)
    position = jnp.arange(PAIR_SPAN, dtype=jnp.int32)
    allowed = (span_docs[:, None] == span_docs[None, :]) & (position[None, :] <= position[:, None])
    query_split = span_queries.reshape(PAIR_SPAN, KV_GROUPS, GROUP_Q, HEAD_DIM)
    grad_split = span_grads.reshape(PAIR_SPAN, KV_GROUPS, GROUP_Q, HEAD_DIM)
    out_list, dq_list, dk_list, dv_list = ([], [], [], [])
    for group_index in range(KV_GROUPS):
        key_group = span_keys[:, group_index * HEAD_DIM:(group_index + 1) * HEAD_DIM]
        value_group = span_values[:, group_index * HEAD_DIM:(group_index + 1) * HEAD_DIM]

        def head_step(running, inputs):
            output, grad_query, grad_key, grad_value = head_pass(inputs[0], inputs[1], key_group, value_group, allowed)
            return ((running[0] + grad_key, running[1] + grad_value), (output, grad_query))
        zeros_init = jnp.zeros((PAIR_SPAN, HEAD_DIM), jnp.float32)
        stacked_in = (jnp.moveaxis(query_split[:, group_index], 1, 0), jnp.moveaxis(grad_split[:, group_index], 1, 0))
        (grad_key, grad_value), (output, grad_query) = lax.scan(head_step, (zeros_init, zeros_init), stacked_in)
        out_list.append(jnp.moveaxis(output, 0, 1).reshape(PAIR_SPAN, GROUP_Q * HEAD_DIM))
        dq_list.append(jnp.moveaxis(grad_query, 0, 1).reshape(PAIR_SPAN, GROUP_Q * HEAD_DIM))
        dk_list.append(grad_key)
        dv_list.append(grad_value)
    return (jnp.concatenate(out_list, axis=1), jnp.concatenate(dq_list, axis=1), jnp.concatenate(dk_list, axis=1), jnp.concatenate(dv_list, axis=1))

def reference(queries, key_heads, value_heads, grad_output, token_logprob, doc_ids, response):
    spans = SEQ // PAIR_SPAN

    def one_span(number):
        return span_pass(queries, key_heads, value_heads, grad_output, doc_ids, number)
    results = lax.map(one_span, jnp.arange(spans, dtype=jnp.int32))
    attention = results[0].reshape(SEQ, HEADS * HEAD_DIM)
    grad_queries = results[1].reshape(SEQ, HEADS * HEAD_DIM)
    grad_keys = results[2].reshape(SEQ, KV_GROUPS * HEAD_DIM)
    grad_values = results[3].reshape(SEQ, KV_GROUPS * HEAD_DIM)
    live = response.astype(jnp.float32)
    doc_sum = jax.ops.segment_sum(token_logprob * live, doc_ids, num_segments=2 * PAIRS)
    doc_count = jax.ops.segment_sum(live, doc_ids, num_segments=2 * PAIRS)
    average = doc_sum / doc_count
    margins = average[0::2] - average[1::2]
    return (attention, grad_queries, grad_keys, grad_values, margins)
```

```python
import math

import jax
import jax.numpy as jnp
from jax import lax
from jax.experimental import pallas as pl
from jax.experimental.pallas import tpu as pltpu
from jax.sharding import PartitionSpec as P

HEAD_DIM = 128
HEADS = 6
PAIR_SPAN = 2048
ROWS = 256
BLOCKS = PAIR_SPAN // ROWS
NEG = -1e30
INV_ROOT = 1.0 / math.sqrt(HEAD_DIM)
SCALE2 = INV_ROOT * math.log2(math.e)

NT = (((1,), (1,)), ((), ()))
TN = (((0,), (0,)), ((), ()))


def dot(a, b, dims=(((1,), (0,)), ((), ()))):
    return lax.dot_general(a, b, dims, preferred_element_type=jnp.float32)


def attend_kernel(
    place, queries, grads, keys, values, attention, grad_queries, grad_kv,
    keys_t, values_t, scores, probs, grad_scores, acc_k, acc_v,
):
    first_row = place[0]
    cut = place[1]
    keys_t[...] = keys[...].T
    values_t[...] = values[...].T
    row = first_row + lax.broadcasted_iota(jnp.int32, (ROWS, ROWS), 0)
    lane = lax.broadcasted_iota(jnp.int32, (ROWS, ROWS), 1)
    start = jnp.where(row >= cut, cut, 0)
    for head in range(HEADS):
        cols = slice(head * HEAD_DIM, (head + 1) * HEAD_DIM)
        query = queries[:, cols]
        grad = grads[:, cols]
        top = None
        for block in range(BLOCKS):
            span = slice(block * ROWS, (block + 1) * ROWS)
            col = lane + block * ROWS
            score = dot(query, keys_t[:, span])
            score = jnp.where((col >= start) & (col <= row), score, NEG)
            scores[:, span] = score
            top = score if top is None else jnp.maximum(top, score)
        row_max = jnp.max(top, axis=1, keepdims=True) * SCALE2
        total = None
        for block in range(BLOCKS):
            span = slice(block * ROWS, (block + 1) * ROWS)
            prob = jnp.exp2(scores[:, span] * SCALE2 - row_max)
            probs[:, span] = prob.astype(jnp.bfloat16)
            total = prob if total is None else total + prob
        inv_total = 1.0 / jnp.sum(total, axis=1, keepdims=True)
        output = (dot(probs[...], values[...]) * inv_total).astype(jnp.bfloat16)
        attention[:, cols] = output
        grad_wide = grad.astype(jnp.float32)
        delta = jnp.sum(grad_wide * output.astype(jnp.float32), axis=1, keepdims=True) * inv_total
        grad_scaled = (grad_wide * inv_total).astype(jnp.bfloat16)
        for block in range(BLOCKS):
            span = slice(block * ROWS, (block + 1) * ROWS)
            grad_prob = dot(grad_scaled, values_t[:, span])
            grad_score = probs[:, span].astype(jnp.float32) * (grad_prob - delta)
            grad_scores[:, span] = grad_score.astype(jnp.bfloat16)
        grad_queries[:, cols] = dot(grad_scores[...], keys[...]) * INV_ROOT
        part_k = dot(grad_scores[...], query, TN)
        part_v = dot(probs[...], grad_scaled, TN)
        if head == 0:
            acc_k[...] = part_k
            acc_v[...] = part_v
        elif head < HEADS - 1:
            acc_k[...] += part_k
            acc_v[...] += part_v
        else:
            grad_kv[:, :HEAD_DIM] = ((acc_k[...] + part_k) * INV_ROOT).astype(jnp.bfloat16)
            grad_kv[:, HEAD_DIM:] = (acc_v[...] + part_v).astype(jnp.bfloat16)


def attend(place, queries, grads, keys, values):
    vmem = pl.BlockSpec(memory_space=pltpu.VMEM)
    width = HEADS * HEAD_DIM
    return pl.pallas_call(
        attend_kernel,
        out_shape=(
            jax.ShapeDtypeStruct((ROWS, width), jnp.bfloat16),
            jax.ShapeDtypeStruct((ROWS, width), jnp.float32),
            jax.ShapeDtypeStruct((PAIR_SPAN, 2 * HEAD_DIM), jnp.bfloat16),
        ),
        in_specs=[pl.BlockSpec(memory_space=pltpu.SMEM), vmem, vmem, vmem, vmem],
        out_specs=(vmem, vmem, vmem),
        scratch_shapes=[
            pltpu.VMEM((HEAD_DIM, PAIR_SPAN), jnp.bfloat16),
            pltpu.VMEM((HEAD_DIM, PAIR_SPAN), jnp.bfloat16),
            pltpu.VMEM((ROWS, PAIR_SPAN), jnp.float32),
            pltpu.VMEM((ROWS, PAIR_SPAN), jnp.bfloat16),
            pltpu.VMEM((ROWS, PAIR_SPAN), jnp.bfloat16),
            pltpu.VMEM((PAIR_SPAN, HEAD_DIM), jnp.float32),
            pltpu.VMEM((PAIR_SPAN, HEAD_DIM), jnp.float32),
        ],
        compiler_params=pltpu.CompilerParams(vmem_limit_bytes=48 * 1024 * 1024),
        cost_estimate=pl.CostEstimate(
            flops=12 * HEADS * ROWS * PAIR_SPAN * HEAD_DIM,
            bytes_accessed=4 * 1024 * 1024,
            transcendentals=HEADS * ROWS * PAIR_SPAN,
        ),
    )(place, queries, grads, keys, values)


def per_device(queries, key_heads, value_heads, grad_output, token_logprob, doc_ids, response):
    groups = [list(range(8)), list(range(8, 16))]
    rank = lax.axis_index("ka") % 8
    odd = (doc_ids & 1).astype(jnp.float32)
    live = response.astype(jnp.float32)
    mine = jnp.stack(
        [
            jnp.sum(token_logprob * live * (1.0 - odd)),
            jnp.sum(token_logprob * live * odd),
            jnp.sum(live * (1.0 - odd)),
            jnp.sum(live * odd),
        ]
    )
    kv = jnp.concatenate([key_heads, value_heads], axis=1)
    kv = lax.all_gather(kv, "ka", axis_index_groups=groups, tiled=True)
    docs = lax.all_gather(doc_ids, "ka", axis_index_groups=groups, tiled=True)
    cut = jnp.sum(1 - (docs & 1)).astype(jnp.int32)
    place = jnp.stack([(rank * ROWS).astype(jnp.int32), cut])
    stats = lax.all_gather(mine, ("pb", "ka"))
    attention, grad_queries, grad_kv = attend(
        place, queries, grad_output, kv[:, :HEAD_DIM], kv[:, HEAD_DIM:]
    )
    grad_kv = lax.psum_scatter(
        grad_kv, "ka", scatter_dimension=0, axis_index_groups=groups, tiled=True
    ).astype(jnp.float32)
    sums = jnp.sum(stats.reshape(-1, 8, 4), axis=1)
    average = sums[:, :2] / sums[:, 2:]
    margins = average[:, 0] - average[:, 1]
    return (attention, grad_queries, grad_kv[:, :HEAD_DIM], grad_kv[:, HEAD_DIM:], margins)


def solution(mesh):
    rows = P(("pb", "ka"), None)
    line = P(("pb", "ka"))
    return jax.shard_map(
        per_device,
        mesh=mesh,
        in_specs=(rows, rows, rows, rows, line, line, line),
        out_specs=(rows, rows, rows, rows, P()),
        check_vma=False,
    )
```

```python
import math

import jax
import jax.numpy as jnp
from jax import lax
from jax.experimental import pallas as pl
from jax.experimental.pallas import tpu as pltpu
from jax.sharding import PartitionSpec as P

HEAD_DIM = 128
HEADS = 6
PAIR_SPAN = 2048
ROWS = 256
BLOCKS = PAIR_SPAN // ROWS
PACKED = 2 * ROWS + 16
NEG = -1e30
INV_ROOT = 1.0 / math.sqrt(HEAD_DIM)
SCALE2 = INV_ROOT * math.log2(math.e)

TN = (((0,), (0,)), ((), ()))
VMEM = pl.BlockSpec(memory_space=pltpu.VMEM)
MIB = 1024 * 1024


def dot(a, b, dims=(((1,), (0,)), ((), ()))):
    return lax.dot_general(a, b, dims, preferred_element_type=jnp.float32)


def pack_kernel(keys, values, logprob, docs, response, packed, sums):
    odd = (docs[...] & 1).astype(jnp.float32)
    even = 1.0 - odd
    live = response[...].astype(jnp.float32)
    scored = logprob[...] * live
    lane = lax.broadcasted_iota(jnp.int32, (1, 128), 1)
    terms = (scored * even, scored * odd, live * even, live * odd)
    line = jnp.zeros((1, 128), jnp.float32)
    for place, term in enumerate(terms):
        line = jnp.where(lane == place, jnp.sum(term, keepdims=True), line)
    sums[...] = jnp.broadcast_to(line[None], sums.shape)
    count = jnp.broadcast_to(jnp.sum(even, keepdims=True), (16, 128)).astype(jnp.bfloat16)
    for copy in range(BLOCKS):
        packed[copy, :ROWS, :] = keys[...]
        packed[copy, ROWS : 2 * ROWS, :] = values[...]
        packed[copy, 2 * ROWS :, :] = count


def pack(keys, values, logprob, docs, response, copies):
    wide = (ROWS // 128, 128)
    return pl.pallas_call(
        pack_kernel,
        out_shape=(
            jax.ShapeDtypeStruct((BLOCKS, PACKED, HEAD_DIM), jnp.bfloat16),
            jax.ShapeDtypeStruct((copies, 8, 128), jnp.float32),
        ),
        in_specs=[VMEM] * 5,
        out_specs=(VMEM, VMEM),
        cost_estimate=pl.CostEstimate(flops=10000, bytes_accessed=2 * MIB, transcendentals=0),
    )(keys, values, logprob.reshape(wide), docs.reshape(wide), response.reshape(wide))


def margin_kernel(sums, margins):
    lane = lax.broadcasted_iota(jnp.int32, (1, 128), 1)
    line = jnp.zeros((1, 128), jnp.float32)
    for pair in range(2):
        total = jnp.sum(sums[pair * BLOCKS : (pair + 1) * BLOCKS, 0, :], axis=0, keepdims=True)
        each = [jnp.sum(jnp.where(lane == at, total, 0.0), keepdims=True) for at in range(4)]
        line = jnp.where(lane == pair, each[0] / each[2] - each[1] / each[3], line)
    margins[...] = jnp.broadcast_to(line[None], margins.shape)


def pair_margins(sums, copies):
    return pl.pallas_call(
        margin_kernel,
        out_shape=jax.ShapeDtypeStruct((copies, 8, 128), jnp.float32),
        in_specs=[VMEM],
        out_specs=VMEM,
        cost_estimate=pl.CostEstimate(flops=10000, bytes_accessed=65536, transcendentals=0),
    )(sums)


def attend_kernel(
    queries, grads, packed, attention, grad_queries, grad_kv,
    keys, values, keys_t, values_t, scores, probs, grad_scores, acc_k, acc_v,
):
    first_row = lax.rem(lax.axis_index("ka"), BLOCKS) * ROWS
    count = packed[0, 2 * ROWS : 2 * ROWS + 16, :].astype(jnp.float32)
    for block in range(BLOCKS):
        span = slice(block * ROWS, (block + 1) * ROWS)
        key = packed[block, :ROWS, :]
        value = packed[block, ROWS : 2 * ROWS, :]
        keys[span, :] = key
        values[span, :] = value
        keys_t[:, span] = key.T
        values_t[:, span] = value.T
        if block:
            count += packed[block, 2 * ROWS : 2 * ROWS + 16, :].astype(jnp.float32)
    cut = count[:1, :1].astype(jnp.int32)
    row = first_row + lax.broadcasted_iota(jnp.int32, (ROWS, ROWS), 0)
    lane = lax.broadcasted_iota(jnp.int32, (ROWS, ROWS), 1)
    start = jnp.where(row >= cut, cut, 0)
    for head in range(HEADS):
        cols = slice(head * HEAD_DIM, (head + 1) * HEAD_DIM)
        query = queries[:, cols]
        grad = grads[:, cols]
        top = None
        for block in range(BLOCKS):
            span = slice(block * ROWS, (block + 1) * ROWS)
            col = lane + block * ROWS
            score = dot(query, keys_t[:, span])
            score = jnp.where((col >= start) & (col <= row), score, NEG)
            scores[:, span] = score
            top = score if top is None else jnp.maximum(top, score)
        row_max = jnp.max(top, axis=1, keepdims=True) * SCALE2
        total = None
        for block in range(BLOCKS):
            span = slice(block * ROWS, (block + 1) * ROWS)
            prob = jnp.exp2(scores[:, span] * SCALE2 - row_max)
            probs[:, span] = prob.astype(jnp.bfloat16)
            total = prob if total is None else total + prob
        inv_total = 1.0 / jnp.sum(total, axis=1, keepdims=True)
        output = (dot(probs[...], values[...]) * inv_total).astype(jnp.bfloat16)
        attention[:, cols] = output
        grad_wide = grad.astype(jnp.float32)
        delta = jnp.sum(grad_wide * output.astype(jnp.float32), axis=1, keepdims=True) * inv_total
        grad_scaled = (grad_wide * inv_total).astype(jnp.bfloat16)
        for block in range(BLOCKS):
            span = slice(block * ROWS, (block + 1) * ROWS)
            grad_prob = dot(grad_scaled, values_t[:, span])
            grad_score = probs[:, span].astype(jnp.float32) * (grad_prob - delta)
            grad_scores[:, span] = grad_score.astype(jnp.bfloat16)
        grad_queries[:, cols] = dot(grad_scores[...], keys[...]) * INV_ROOT
        part_k = dot(grad_scores[...], query, TN)
        part_v = dot(probs[...], grad_scaled, TN)
        if head == 0:
            acc_k[...] = part_k
            acc_v[...] = part_v
        elif head < HEADS - 1:
            acc_k[...] += part_k
            acc_v[...] += part_v
        else:
            grad_kv[:, :HEAD_DIM] = ((acc_k[...] + part_k) * INV_ROOT).astype(jnp.bfloat16)
            grad_kv[:, HEAD_DIM:] = (acc_v[...] + part_v).astype(jnp.bfloat16)


def attend(queries, grads, packed):
    width = HEADS * HEAD_DIM
    return pl.pallas_call(
        attend_kernel,
        out_shape=(
            jax.ShapeDtypeStruct((ROWS, width), jnp.bfloat16),
            jax.ShapeDtypeStruct((ROWS, width), jnp.float32),
            jax.ShapeDtypeStruct((PAIR_SPAN, 2 * HEAD_DIM), jnp.bfloat16),
        ),
        in_specs=[VMEM] * 3,
        out_specs=(VMEM,) * 3,
        scratch_shapes=[
            pltpu.VMEM((PAIR_SPAN, HEAD_DIM), jnp.bfloat16),
            pltpu.VMEM((PAIR_SPAN, HEAD_DIM), jnp.bfloat16),
            pltpu.VMEM((HEAD_DIM, PAIR_SPAN), jnp.bfloat16),
            pltpu.VMEM((HEAD_DIM, PAIR_SPAN), jnp.bfloat16),
            pltpu.VMEM((ROWS, PAIR_SPAN), jnp.float32),
            pltpu.VMEM((ROWS, PAIR_SPAN), jnp.bfloat16),
            pltpu.VMEM((ROWS, PAIR_SPAN), jnp.bfloat16),
            pltpu.VMEM((PAIR_SPAN, HEAD_DIM), jnp.float32),
            pltpu.VMEM((PAIR_SPAN, HEAD_DIM), jnp.float32),
        ],
        compiler_params=pltpu.CompilerParams(vmem_limit_bytes=32 * MIB),
        cost_estimate=pl.CostEstimate(
            flops=12 * HEADS * ROWS * PAIR_SPAN * HEAD_DIM,
            bytes_accessed=4 * MIB,
            transcendentals=HEADS * ROWS * PAIR_SPAN,
        ),
    )(queries, grads, packed)


def collect_kernel(parts, grad_keys, grad_values):
    total = parts[0].astype(jnp.float32)
    for block in range(1, BLOCKS):
        total += parts[block].astype(jnp.float32)
    grad_keys[...] = total[:, :HEAD_DIM]
    grad_values[...] = total[:, HEAD_DIM:]


def collect(parts):
    shape = jax.ShapeDtypeStruct((ROWS, HEAD_DIM), jnp.float32)
    return pl.pallas_call(
        collect_kernel,
        out_shape=(shape, shape),
        in_specs=[VMEM],
        out_specs=(VMEM, VMEM),
        cost_estimate=pl.CostEstimate(flops=MIB, bytes_accessed=2 * MIB, transcendentals=0),
    )(parts)


def per_device(queries, key_heads, value_heads, grad_output, token_logprob, doc_ids, response):
    groups = [list(range(8)), list(range(8, 16))]
    packed, sums = pack(key_heads, value_heads, token_logprob, doc_ids, response, 16)
    packed = lax.all_to_all(packed, "ka", 0, 0, axis_index_groups=groups, tiled=True)
    sums = lax.all_to_all(sums, "ka", 0, 0, tiled=True)
    margins = lax.all_to_all(pair_margins(sums, 16), "pb", 0, 0, tiled=True)
    attention, grad_queries, grad_kv = attend(queries, grad_output, packed)
    parts = grad_kv.reshape(BLOCKS, ROWS, 2 * HEAD_DIM)
    parts = lax.all_to_all(parts, "ka", 0, 0, axis_index_groups=groups, tiled=True)
    grad_keys, grad_values = collect(parts)
    return (attention, grad_queries, grad_keys, grad_values, margins[:, 0, :2].reshape(-1))


def solution(mesh):
    rows = P(("pb", "ka"), None)
    line = P(("pb", "ka"))
    return jax.shard_map(
        per_device,
        mesh=mesh,
        in_specs=(rows, rows, rows, rows, line, line, line),
        out_specs=(rows, rows, rows, rows, P()),
        check_vma=False,
    )
```

```python
import math

import jax
import jax.numpy as jnp
from jax import lax
from jax.experimental import pallas as pl
from jax.experimental.pallas import tpu as pltpu
from jax.sharding import PartitionSpec as P

HEAD_DIM = 128
HEADS = 6
PAIR_SPAN = 2048
ROWS = 256
BLOCKS = PAIR_SPAN // ROWS
PACKED = 2 * ROWS + 16
CHIPS = 4
NEG = -1e30
INV_ROOT = 1.0 / math.sqrt(HEAD_DIM)
SCALE2 = INV_ROOT * math.log2(math.e)

TN = (((0,), (0,)), ((), ()))
VMEM = pl.BlockSpec(memory_space=pltpu.VMEM)
MIB = 1024 * 1024


def dot(a, b, dims=(((1,), (0,)), ((), ()))):
    return lax.dot_general(a, b, dims, preferred_element_type=jnp.float32)


def pack_kernel(keys, values, logprob, docs, response, packed, sums):
    odd = (docs[...] & 1).astype(jnp.float32)
    even = 1.0 - odd
    live = response[...].astype(jnp.float32)
    scored = logprob[...] * live
    lane = lax.broadcasted_iota(jnp.int32, (1, 128), 1)
    terms = (scored * even, scored * odd, live * even, live * odd)
    line = jnp.zeros((1, 128), jnp.float32)
    for place, term in enumerate(terms):
        line = jnp.where(lane == place, jnp.sum(term, keepdims=True), line)
    sums[...] = jnp.broadcast_to(line, sums.shape)
    count = jnp.broadcast_to(jnp.sum(even, keepdims=True), (16, 128)).astype(jnp.bfloat16)
    for copy in range(CHIPS):
        packed[copy, :ROWS, :] = keys[...]
        packed[copy, ROWS : 2 * ROWS, :] = values[...]
        packed[copy, 2 * ROWS :, :] = count


def pack(keys, values, logprob, docs, response):
    wide = (ROWS // 128, 128)
    return pl.pallas_call(
        pack_kernel,
        out_shape=(
            jax.ShapeDtypeStruct((CHIPS, PACKED, HEAD_DIM), jnp.bfloat16),
            jax.ShapeDtypeStruct((8, 128), jnp.float32),
        ),
        in_specs=[VMEM] * 5,
        out_specs=(VMEM, VMEM),
        cost_estimate=pl.CostEstimate(flops=10000, bytes_accessed=2 * MIB, transcendentals=0),
    )(keys, values, logprob.reshape(wide), docs.reshape(wide), response.reshape(wide))


def margin_kernel(sums, margins):
    lane = lax.broadcasted_iota(jnp.int32, (1, 128), 1)
    line = jnp.zeros((1, 128), jnp.float32)
    for pair in range(2):
        total = jnp.sum(sums[pair * BLOCKS : (pair + 1) * BLOCKS, 0, :], axis=0, keepdims=True)
        each = [jnp.sum(jnp.where(lane == at, total, 0.0), keepdims=True) for at in range(4)]
        line = jnp.where(lane == pair, each[0] / each[2] - each[1] / each[3], line)
    margins[...] = jnp.broadcast_to(line, margins.shape)


def pair_margins(sums):
    return pl.pallas_call(
        margin_kernel,
        out_shape=jax.ShapeDtypeStruct((8, 128), jnp.float32),
        in_specs=[VMEM],
        out_specs=VMEM,
        cost_estimate=pl.CostEstimate(flops=10000, bytes_accessed=65536, transcendentals=0),
    )(sums)


def attend_kernel(
    queries, grads, same_core, other_core, attention, grad_queries, same_grads, other_grads,
    keys, values, keys_t, values_t, scores, probs, grad_scores, acc_k, acc_v,
):
    place = lax.axis_index("ka")
    core = lax.rem(place, 2)
    first_row = lax.rem(place, BLOCKS) * ROWS
    sources = [(ref, chip) for ref in (same_core, other_core) for chip in range(CHIPS)]
    firsts = [2 * chip * ROWS + core * ROWS for chip in range(CHIPS)]
    firsts += [2 * chip * ROWS + (1 - core) * ROWS for chip in range(CHIPS)]
    count = None
    for block, (ref, chip) in enumerate(sources):
        span = slice(block * ROWS, (block + 1) * ROWS)
        key = ref[chip, :ROWS, :]
        value = ref[chip, ROWS : 2 * ROWS, :]
        keys[span, :] = key
        values[span, :] = value
        keys_t[:, span] = key.T
        values_t[:, span] = value.T
        term = ref[chip, 2 * ROWS : 2 * ROWS + 16, :].astype(jnp.float32)
        count = term if count is None else count + term
    cut = count[:1, :1].astype(jnp.int32)
    row = first_row + lax.broadcasted_iota(jnp.int32, (ROWS, ROWS), 0)
    lane = lax.broadcasted_iota(jnp.int32, (ROWS, ROWS), 1)
    start = jnp.where(row >= cut, cut, 0)
    for head in range(HEADS):
        cols = slice(head * HEAD_DIM, (head + 1) * HEAD_DIM)
        query = queries[:, cols]
        grad = grads[:, cols]
        top = None
        for block in range(BLOCKS):
            span = slice(block * ROWS, (block + 1) * ROWS)
            col = lane + firsts[block]
            score = dot(query, keys_t[:, span])
            score = jnp.where((col >= start) & (col <= row), score, NEG)
            scores[:, span] = score
            top = score if top is None else jnp.maximum(top, score)
        row_max = jnp.max(top, axis=1, keepdims=True) * SCALE2
        total = None
        for block in range(BLOCKS):
            span = slice(block * ROWS, (block + 1) * ROWS)
            prob = jnp.exp2(scores[:, span] * SCALE2 - row_max)
            probs[:, span] = prob.astype(jnp.bfloat16)
            total = prob if total is None else total + prob
        inv_total = 1.0 / jnp.sum(total, axis=1, keepdims=True)
        output = (dot(probs[...], values[...]) * inv_total).astype(jnp.bfloat16)
        attention[:, cols] = output
        grad_wide = grad.astype(jnp.float32)
        delta = jnp.sum(grad_wide * output.astype(jnp.float32), axis=1, keepdims=True) * inv_total
        grad_scaled = (grad_wide * inv_total).astype(jnp.bfloat16)
        for block in range(BLOCKS):
            span = slice(block * ROWS, (block + 1) * ROWS)
            grad_prob = dot(grad_scaled, values_t[:, span])
            grad_score = probs[:, span].astype(jnp.float32) * (grad_prob - delta)
            grad_scores[:, span] = grad_score.astype(jnp.bfloat16)
        grad_queries[:, cols] = dot(grad_scores[...], keys[...]) * INV_ROOT
        part_k = dot(grad_scores[...], query, TN)
        part_v = dot(probs[...], grad_scaled, TN)
        if head == 0:
            acc_k[...] = part_k
            acc_v[...] = part_v
        elif head < HEADS - 1:
            acc_k[...] += part_k
            acc_v[...] += part_v
        else:
            for block in range(BLOCKS):
                span = slice(block * ROWS, (block + 1) * ROWS)
                ref = same_grads if block < CHIPS else other_grads
                chip = block % CHIPS
                grad_key = (acc_k[span, :] + part_k[span, :]) * INV_ROOT
                ref[chip, :, :HEAD_DIM] = grad_key.astype(jnp.bfloat16)
                ref[chip, :, HEAD_DIM:] = (acc_v[span, :] + part_v[span, :]).astype(jnp.bfloat16)


def attend(queries, grads, same_core, other_core):
    width = HEADS * HEAD_DIM
    return pl.pallas_call(
        attend_kernel,
        out_shape=(
            jax.ShapeDtypeStruct((ROWS, width), jnp.bfloat16),
            jax.ShapeDtypeStruct((ROWS, width), jnp.float32),
            jax.ShapeDtypeStruct((CHIPS, ROWS, 2 * HEAD_DIM), jnp.bfloat16),
            jax.ShapeDtypeStruct((CHIPS, ROWS, 2 * HEAD_DIM), jnp.bfloat16),
        ),
        in_specs=[VMEM] * 4,
        out_specs=(VMEM,) * 4,
        scratch_shapes=[
            pltpu.VMEM((PAIR_SPAN, HEAD_DIM), jnp.bfloat16),
            pltpu.VMEM((PAIR_SPAN, HEAD_DIM), jnp.bfloat16),
            pltpu.VMEM((HEAD_DIM, PAIR_SPAN), jnp.bfloat16),
            pltpu.VMEM((HEAD_DIM, PAIR_SPAN), jnp.bfloat16),
            pltpu.VMEM((ROWS, PAIR_SPAN), jnp.float32),
            pltpu.VMEM((ROWS, PAIR_SPAN), jnp.bfloat16),
            pltpu.VMEM((ROWS, PAIR_SPAN), jnp.bfloat16),
            pltpu.VMEM((PAIR_SPAN, HEAD_DIM), jnp.float32),
            pltpu.VMEM((PAIR_SPAN, HEAD_DIM), jnp.float32),
        ],
        compiler_params=pltpu.CompilerParams(vmem_limit_bytes=32 * MIB),
        cost_estimate=pl.CostEstimate(
            flops=12 * HEADS * ROWS * PAIR_SPAN * HEAD_DIM,
            bytes_accessed=4 * MIB,
            transcendentals=HEADS * ROWS * PAIR_SPAN,
        ),
    )(queries, grads, same_core, other_core)


def collect_kernel(parts, grad_keys, grad_values):
    total = parts[0].astype(jnp.float32)
    for block in range(1, CHIPS):
        total += parts[block].astype(jnp.float32)
    grad_keys[...] = total[:, :HEAD_DIM]
    grad_values[...] = total[:, HEAD_DIM:]


def collect(parts):
    shape = jax.ShapeDtypeStruct((ROWS, HEAD_DIM), jnp.float32)
    return pl.pallas_call(
        collect_kernel,
        out_shape=(shape, shape),
        in_specs=[VMEM],
        out_specs=(VMEM, VMEM),
        cost_estimate=pl.CostEstimate(flops=MIB, bytes_accessed=2 * MIB, transcendentals=0),
    )(parts)


def per_device(queries, key_heads, value_heads, grad_output, token_logprob, doc_ids, response):
    rings = [[half * 8 + 2 * chip + core for chip in range(CHIPS)] for half in (0, 1) for core in (0, 1)]
    swap = [(place, place ^ 1) for place in range(16)]
    packed, sums = pack(key_heads, value_heads, token_logprob, doc_ids, response)
    same_core = lax.all_to_all(packed, "ka", 0, 0, axis_index_groups=rings, tiled=True)
    sums = lax.all_gather(sums, "ka")
    margins = lax.all_gather(pair_margins(sums), "pb")
    other_core = lax.ppermute(same_core, "ka", swap)
    attention, grad_queries, same_grads, other_grads = attend(
        queries, grad_output, same_core, other_core
    )
    same_grads = same_grads + lax.ppermute(other_grads, "ka", swap)
    parts = lax.all_to_all(same_grads, "ka", 0, 0, axis_index_groups=rings, tiled=True)
    grad_keys, grad_values = collect(parts)
    return (attention, grad_queries, grad_keys, grad_values, margins[:, 0, :2].reshape(-1))


def solution(mesh):
    rows = P(("pb", "ka"), None)
    line = P(("pb", "ka"))
    return jax.shard_map(
        per_device,
        mesh=mesh,
        in_specs=(rows, rows, rows, rows, line, line, line),
        out_specs=(rows, rows, rows, rows, P()),
        check_vma=False,
    )
```

```python
import math

import jax
import jax.numpy as jnp
from jax import lax
from jax.experimental import pallas as pl
from jax.experimental.pallas import tpu as pltpu
from jax.sharding import PartitionSpec as P

HEAD_DIM = 128
HEADS = 6
PAIR_SPAN = 2048
ROWS = 256
BLOCKS = PAIR_SPAN // ROWS
CHIPS = 4
PAIRS = 32
PACKED = 2 * ROWS + 16
NEG = -1e30
INV_ROOT = 1.0 / math.sqrt(HEAD_DIM)
SCALE2 = INV_ROOT * math.log2(math.e)

VMEM = pl.BlockSpec(memory_space=pltpu.VMEM)
MIB = 1024 * 1024


def dot(a, b):
    return jnp.dot(a, b, preferred_element_type=jnp.float32)


def pack_kernel(keys, values, logprob, docs, response, packed, sums):
    pair = lax.axis_index("pb") * 2 + lax.axis_index("ka") // BLOCKS
    odd = (docs[...] & 1).astype(jnp.float32)
    even = 1.0 - odd
    live = response[...].astype(jnp.float32)
    scored = logprob[...] * live
    row = lax.broadcasted_iota(jnp.int32, (8, 128), 0)
    lane = lax.broadcasted_iota(jnp.int32, (8, 128), 1)
    table = jnp.zeros((8, 128), jnp.float32)
    for place, term in enumerate((scored * even, scored * odd, live * even, live * odd)):
        here = (row == place) & (lane == pair)
        table = jnp.where(here, jnp.sum(term, keepdims=True), table)
    sums[...] = table
    packed[:ROWS, :] = keys[...]
    packed[ROWS : 2 * ROWS, :] = values[...]
    count = jnp.broadcast_to(jnp.sum(even, keepdims=True), (16, 128))
    packed[2 * ROWS :, :] = count.astype(jnp.bfloat16)


def pack(keys, values, logprob, docs, response):
    wide = (ROWS // 128, 128)
    return pl.pallas_call(
        pack_kernel,
        out_shape=(
            jax.ShapeDtypeStruct((PACKED, HEAD_DIM), jnp.bfloat16),
            jax.ShapeDtypeStruct((8, 128), jnp.float32),
        ),
        in_specs=[VMEM] * 5,
        out_specs=(VMEM, VMEM),
        cost_estimate=pl.CostEstimate(flops=10000, bytes_accessed=MIB // 2, transcendentals=0),
    )(keys, values, logprob.reshape(wide), docs.reshape(wide), response.reshape(wide))


def attend_kernel(
    queries, grads, own, near, far, opposite, own_s, near_s, far_s, opposite_s,
    attention, grad_queries, same_grads, other_grads,
    keys, values, keys_t, values_t, bias, scores, probs, grad_scores, acc_k, acc_v,
):
    place = lax.axis_index("ka")
    core = lax.rem(place, 2)
    chip = lax.rem(place // 2, CHIPS)
    step = 1 - 2 * core
    chips = [chip, chip - step, chip + step, chip + 2, chip, chip + step, chip - step, chip + 2]
    first_row = lax.rem(place, BLOCKS) * ROWS
    count = None
    for block, ref in enumerate((own, near, far, opposite, own_s, near_s, far_s, opposite_s)):
        span = slice(block * ROWS, (block + 1) * ROWS)
        key = ref[:ROWS, :]
        value = ref[ROWS : 2 * ROWS, :]
        keys[span, :] = key
        values[span, :] = value
        keys_t[:, span] = key.T
        values_t[:, span] = value.T
        term = ref[2 * ROWS :, :].astype(jnp.float32)
        count = term if count is None else count + term
    cut = count[:1, :1].astype(jnp.int32)
    row = first_row + lax.broadcasted_iota(jnp.int32, (ROWS, ROWS), 0)
    lane = lax.broadcasted_iota(jnp.int32, (ROWS, ROWS), 1)
    start = jnp.where(row >= cut, cut, 0)
    for block in range(BLOCKS):
        span = slice(block * ROWS, (block + 1) * ROWS)
        side = core if block < CHIPS else 1 - core
        col = lane + (lax.rem(chips[block] + CHIPS, CHIPS) * 2 + side) * ROWS
        bias[:, span] = jnp.where((col >= start) & (col <= row), 0.0, NEG)
    for head in range(HEADS):
        cols = slice(head * HEAD_DIM, (head + 1) * HEAD_DIM)
        score_ref, prob_ref, grad_ref = (ref.at[head % 2] for ref in (scores, probs, grad_scores))
        query = queries[:, cols]
        grad = grads[:, cols]
        top = None
        for block in range(BLOCKS):
            span = slice(block * ROWS, (block + 1) * ROWS)
            score = dot(query, keys_t[:, span]) + bias[:, span]
            score_ref[:, span] = score
            top = score if top is None else jnp.maximum(top, score)
        row_max = jnp.max(top, axis=1, keepdims=True) * SCALE2
        total = None
        for block in range(BLOCKS):
            span = slice(block * ROWS, (block + 1) * ROWS)
            prob = jnp.exp2(score_ref[:, span] * SCALE2 - row_max)
            prob_ref[:, span] = prob.astype(jnp.bfloat16)
            total = prob if total is None else total + prob
        inv_total = 1.0 / jnp.sum(total, axis=1, keepdims=True)
        output = (dot(prob_ref[...], values[...]) * inv_total).astype(jnp.bfloat16)
        attention[:, cols] = output
        grad_wide = grad.astype(jnp.float32)
        delta = jnp.sum(grad_wide * output.astype(jnp.float32), axis=1, keepdims=True) * inv_total
        grad_scaled = (grad_wide * inv_total).astype(jnp.bfloat16)
        for block in range(BLOCKS):
            span = slice(block * ROWS, (block + 1) * ROWS)
            grad_prob = dot(grad_scaled, values_t[:, span])
            grad_score = prob_ref[:, span].astype(jnp.float32) * (grad_prob - delta)
            grad_ref[:, span] = grad_score.astype(jnp.bfloat16)
        grad_queries[:, cols] = dot(grad_ref[...], keys[...]) * INV_ROOT
        query_t = query.T
        grad_t = grad_scaled.T
        for block in range(BLOCKS):
            span = slice(block * ROWS, (block + 1) * ROWS)
            part_k = dot(query_t, grad_ref[:, span])
            part_v = dot(grad_t, prob_ref[:, span])
            if head:
                part_k += acc_k[:, span]
                part_v += acc_v[:, span]
            if head < HEADS - 1:
                acc_k[:, span] = part_k
                acc_v[:, span] = part_v
            else:
                out = same_grads if block < CHIPS else other_grads
                out[block % CHIPS, :, :HEAD_DIM] = (part_k * INV_ROOT).astype(jnp.bfloat16).T
                out[block % CHIPS, :, HEAD_DIM:] = part_v.astype(jnp.bfloat16).T


def attend(queries, grads, blocks):
    width = HEADS * HEAD_DIM
    part = jax.ShapeDtypeStruct((CHIPS, ROWS, 2 * HEAD_DIM), jnp.bfloat16)
    return pl.pallas_call(
        attend_kernel,
        out_shape=(
            jax.ShapeDtypeStruct((ROWS, width), jnp.bfloat16),
            jax.ShapeDtypeStruct((ROWS, width), jnp.float32),
            part,
            part,
        ),
        in_specs=[VMEM] * (2 + BLOCKS),
        out_specs=(VMEM,) * 4,
        scratch_shapes=[
            pltpu.VMEM((PAIR_SPAN, HEAD_DIM), jnp.bfloat16),
            pltpu.VMEM((PAIR_SPAN, HEAD_DIM), jnp.bfloat16),
            pltpu.VMEM((HEAD_DIM, PAIR_SPAN), jnp.bfloat16),
            pltpu.VMEM((HEAD_DIM, PAIR_SPAN), jnp.bfloat16),
            pltpu.VMEM((ROWS, PAIR_SPAN), jnp.float32),
            pltpu.VMEM((2, ROWS, PAIR_SPAN), jnp.float32),
            pltpu.VMEM((2, ROWS, PAIR_SPAN), jnp.bfloat16),
            pltpu.VMEM((2, ROWS, PAIR_SPAN), jnp.bfloat16),
            pltpu.VMEM((HEAD_DIM, PAIR_SPAN), jnp.float32),
            pltpu.VMEM((HEAD_DIM, PAIR_SPAN), jnp.float32),
        ],
        compiler_params=pltpu.CompilerParams(vmem_limit_bytes=32 * MIB),
        cost_estimate=pl.CostEstimate(
            flops=12 * HEADS * ROWS * PAIR_SPAN * HEAD_DIM,
            bytes_accessed=4 * MIB,
            transcendentals=HEADS * ROWS * PAIR_SPAN,
        ),
    )(queries, grads, *blocks)


def collect_kernel(own, near, far, grad_keys, grad_values):
    total = own[...].astype(jnp.float32) + near[...].astype(jnp.float32)
    total += far[...].astype(jnp.float32)
    grad_keys[...] = total[:, :HEAD_DIM]
    grad_values[...] = total[:, HEAD_DIM:]


def collect(own, near, far):
    shape = jax.ShapeDtypeStruct((ROWS, HEAD_DIM), jnp.float32)
    return pl.pallas_call(
        collect_kernel,
        out_shape=(shape, shape),
        in_specs=[VMEM] * 3,
        out_specs=(VMEM, VMEM),
        cost_estimate=pl.CostEstimate(flops=MIB, bytes_accessed=MIB, transcendentals=0),
    )(own, near, far)


def at(half, chip, core):
    return half * 8 + (chip % CHIPS) * 2 + core


def per_device(queries, key_heads, value_heads, grad_output, token_logprob, doc_ids, response):
    spots = [(half, chip, core) for half in (0, 1) for chip in range(CHIPS) for core in (0, 1)]
    ahead = [(at(h, x, k), at(h, x + 1 - 2 * k, k)) for h, x, k in spots]
    back = [(there, here) for here, there in ahead]
    swap = [(place, place ^ 1) for place in range(16)]

    own, sums = pack(key_heads, value_heads, token_logprob, doc_ids, response)
    near = lax.ppermute(own, "ka", ahead)
    far = lax.ppermute(own, "ka", back)
    own_s = lax.ppermute(own, "ka", swap)
    opposite = lax.ppermute(near, "ka", ahead)
    near_s = lax.ppermute(near, "ka", swap)
    far_s = lax.ppermute(far, "ka", swap)
    opposite_s = lax.ppermute(opposite, "ka", swap)

    for bit in (1, 2, 4, 8):
        sums = sums + lax.ppermute(sums, "pb", [(place, place ^ bit) for place in range(16)])
    queries, sums = lax.optimization_barrier((queries, sums))

    blocks = (own, near, far, opposite, own_s, near_s, far_s, opposite_s)
    attention, grad_queries, same_grads, other_grads = attend(queries, grad_output, blocks)
    other_grads, sums = lax.optimization_barrier((other_grads, sums))
    for bit in (8, 1, 2, 6):
        sums = sums + lax.ppermute(sums, "ka", [(place, place ^ bit) for place in range(16)])
    margins = (sums[0] / sums[2] - sums[1] / sums[3])[:PAIRS]
    same_grads = same_grads + lax.ppermute(other_grads, "ka", swap)
    far_part = lax.ppermute(same_grads[2], "ka", ahead)
    passed = lax.ppermute(same_grads[3], "ka", back)
    near_part = lax.ppermute(same_grads[1] + passed, "ka", back)
    grad_keys, grad_values = collect(same_grads[0], near_part, far_part)
    return (attention, grad_queries, grad_keys, grad_values, margins)


def solution(mesh):
    rows = P(("pb", "ka"), None)
    line = P(("pb", "ka"))
    return jax.shard_map(
        per_device,
        mesh=mesh,
        in_specs=(rows, rows, rows, rows, line, line, line),
        out_specs=(rows, rows, rows, rows, P()),
        check_vma=False,
    )
```

```python
import math

import jax
import jax.numpy as jnp
from jax import lax
from jax.experimental import pallas as pl
from jax.experimental.pallas import tpu as pltpu
from jax.sharding import PartitionSpec as P

HEAD_DIM = 128
HEADS = 6
PAIR_SPAN = 2048
ROWS = 256
BLOCKS = PAIR_SPAN // ROWS
CHIPS = 4
PAIRS = 32
PACKED = 2 * ROWS + 16
NEG = -1e30
INV_ROOT = 1.0 / math.sqrt(HEAD_DIM)
SCALE2 = INV_ROOT * math.log2(math.e)

VMEM = pl.BlockSpec(memory_space=pltpu.VMEM)
MIB = 1024 * 1024


def dot(a, b):
    return jnp.dot(a, b, preferred_element_type=jnp.float32)


def split(value):
    high = value.astype(jnp.bfloat16).astype(jnp.float32)
    middle = (value - high).astype(jnp.bfloat16).astype(jnp.float32)
    return high, middle, value - high - middle


def pack_kernel(keys, values, logprob, docs, response, packed):
    odd = (docs[...] & 1).astype(jnp.float32)
    even = 1.0 - odd
    live = response[...].astype(jnp.float32)
    scored = logprob[...] * live
    first, second, first_live, second_live, count = (
        jnp.sum(term, keepdims=True)
        for term in (scored * even, scored * odd, live * even, live * odd, even)
    )
    terms = (*split(first), *split(second), first_live, second_live, count)
    lane = lax.broadcasted_iota(jnp.int32, (16, HEAD_DIM), 1)
    table = jnp.zeros((16, HEAD_DIM), jnp.float32)
    for place, term in enumerate(terms):
        table = jnp.where(lane == place, term, table)
    packed[:ROWS, :] = keys[...]
    packed[ROWS : 2 * ROWS, :] = values[...]
    packed[2 * ROWS :, :] = table.astype(jnp.bfloat16)


def pack(keys, values, logprob, docs, response):
    wide = (ROWS // 128, 128)
    return pl.pallas_call(
        pack_kernel,
        out_shape=jax.ShapeDtypeStruct((PACKED, HEAD_DIM), jnp.bfloat16),
        in_specs=[VMEM] * 5,
        out_specs=VMEM,
        cost_estimate=pl.CostEstimate(flops=10000, bytes_accessed=MIB // 2, transcendentals=0),
    )(keys, values, logprob.reshape(wide), docs.reshape(wide), response.reshape(wide))


def spans():
    return [(block, slice(block * ROWS, (block + 1) * ROWS)) for block in range(BLOCKS)]


def attend_kernel(
    queries, grads, own, near, far, opposite, own_s, near_s, far_s, opposite_s,
    attention, grad_queries, own_part, near_part, far_part, opposite_part, swap_parts,
    opposite_s_part, margin,
    keys, values, keys_t, values_t, bias, scores, probs, grad_scores, acc_k, acc_v,
):
    place = lax.axis_index("ka")
    core = lax.rem(place, 2)
    chip = lax.rem(place // 2, CHIPS)
    step = 1 - 2 * core
    chips = [chip, chip - step, chip + step, chip + 2, chip, chip + step, chip - step, chip + 2]
    first_row = lax.rem(place, BLOCKS) * ROWS
    blocks = (own, near, far, opposite, own_s, near_s, far_s, opposite_s)
    parts = (
        own_part, near_part, far_part, opposite_part,
        swap_parts.at[0], swap_parts.at[1], swap_parts.at[2], opposite_s_part,
    )
    totals = None
    for block, span in spans():
        key = blocks[block][:ROWS, :]
        value = blocks[block][ROWS : 2 * ROWS, :]
        keys[span, :] = key
        values[span, :] = value
        keys_t[:, span] = key.T
        values_t[:, span] = value.T
        term = blocks[block][2 * ROWS :, :].astype(jnp.float32)
        totals = term if totals is None else totals + term
    totals = totals[:8, :]
    wide = lax.broadcasted_iota(jnp.int32, (8, HEAD_DIM), 1)

    def total_of(low, high):
        chosen = jnp.where((wide >= low) & (wide < high), totals, 0.0)
        return jnp.sum(chosen, axis=1, keepdims=True)

    pair = lax.axis_index("pb") * 2 + place // BLOCKS
    value = total_of(0, 3) / total_of(6, 7) - total_of(3, 6) / total_of(7, 8)
    margin[...] = jnp.where(wide == pair, value, 0.0)
    cut = total_of(8, 9)[:1, :1].astype(jnp.int32)
    row = first_row + lax.broadcasted_iota(jnp.int32, (ROWS, ROWS), 0)
    lane = lax.broadcasted_iota(jnp.int32, (ROWS, ROWS), 1)
    start = jnp.where(row >= cut, cut, 0)
    for block, span in spans():
        side = core if block < CHIPS else 1 - core
        col = lane + (lax.rem(chips[block] + CHIPS, CHIPS) * 2 + side) * ROWS
        bias[:, span] = jnp.where((col >= start) & (col <= row), 0.0, NEG)

    columns = [slice(head * HEAD_DIM, (head + 1) * HEAD_DIM) for head in range(HEADS)]

    def score_step(head, span, top):
        score = dot(queries[:, columns[head]], keys_t[:, span]) + bias[:, span]
        scores[head % 2, :, span] = score
        return score if top is None else jnp.maximum(top, score)

    def prob_step(head, span, row_max, total):
        prob = jnp.exp2(scores[head % 2, :, span] * SCALE2 - row_max)
        probs[head % 2, :, span] = prob.astype(jnp.bfloat16)
        return prob if total is None else total + prob

    def max_of(top):
        return jnp.max(top, axis=1, keepdims=True) * SCALE2

    top = total = None
    for block, span in spans():
        top = score_step(0, span, top)
    row_max = max_of(top)
    for block, span in spans():
        total = prob_step(0, span, row_max, total)
    for head in range(HEADS):
        slot = head % 2
        query = queries[:, columns[head]]
        inv_total = 1.0 / jnp.sum(total, axis=1, keepdims=True)
        output = (dot(probs[slot], values[...]) * inv_total).astype(jnp.bfloat16)
        attention[:, columns[head]] = output
        grad_wide = grads[:, columns[head]].astype(jnp.float32)
        delta = jnp.sum(grad_wide * output.astype(jnp.float32), axis=1, keepdims=True) * inv_total
        grad_scaled = (grad_wide * inv_total).astype(jnp.bfloat16)
        top = total = None
        for block, span in spans():
            grad_prob = dot(grad_scaled, values_t[:, span])
            if head < HEADS - 1:
                top = score_step(head + 1, span, top)
            grad_score = probs[slot, :, span].astype(jnp.float32) * (grad_prob - delta)
            grad_scores[slot, :, span] = grad_score.astype(jnp.bfloat16)
        if head < HEADS - 1:
            row_max = max_of(top)
        query_t = query.T
        grad_t = grad_scaled.T
        for block, span in spans():
            part_k = dot(query_t, grad_scores[slot, :, span])
            part_v = dot(grad_t, probs[slot, :, span])
            if head < HEADS - 1:
                total = prob_step(head + 1, span, row_max, total)
            if head:
                part_k += acc_k[:, span]
                part_v += acc_v[:, span]
            if head < HEADS - 1:
                acc_k[:, span] = part_k
                acc_v[:, span] = part_v
            else:
                parts[block][:, :HEAD_DIM] = (part_k * INV_ROOT).astype(jnp.bfloat16).T
                parts[block][:, HEAD_DIM:] = part_v.astype(jnp.bfloat16).T
        grad_queries[:, columns[head]] = dot(grad_scores[slot], keys[...]) * INV_ROOT


def attend(queries, grads, blocks):
    width = HEADS * HEAD_DIM
    part = jax.ShapeDtypeStruct((ROWS, 2 * HEAD_DIM), jnp.bfloat16)
    return pl.pallas_call(
        attend_kernel,
        out_shape=(
            jax.ShapeDtypeStruct((ROWS, width), jnp.bfloat16),
            jax.ShapeDtypeStruct((ROWS, width), jnp.float32),
            part,
            part,
            part,
            part,
            jax.ShapeDtypeStruct((3, ROWS, 2 * HEAD_DIM), jnp.bfloat16),
            part,
            jax.ShapeDtypeStruct((8, HEAD_DIM), jnp.float32),
        ),
        in_specs=[VMEM] * (2 + BLOCKS),
        out_specs=(VMEM,) * 9,
        scratch_shapes=[
            pltpu.VMEM((PAIR_SPAN, HEAD_DIM), jnp.bfloat16),
            pltpu.VMEM((PAIR_SPAN, HEAD_DIM), jnp.bfloat16),
            pltpu.VMEM((HEAD_DIM, PAIR_SPAN), jnp.bfloat16),
            pltpu.VMEM((HEAD_DIM, PAIR_SPAN), jnp.bfloat16),
            pltpu.VMEM((ROWS, PAIR_SPAN), jnp.float32),
            pltpu.VMEM((2, ROWS, PAIR_SPAN), jnp.float32),
            pltpu.VMEM((2, ROWS, PAIR_SPAN), jnp.bfloat16),
            pltpu.VMEM((2, ROWS, PAIR_SPAN), jnp.bfloat16),
            pltpu.VMEM((HEAD_DIM, PAIR_SPAN), jnp.float32),
            pltpu.VMEM((HEAD_DIM, PAIR_SPAN), jnp.float32),
        ],
        compiler_params=pltpu.CompilerParams(vmem_limit_bytes=32 * MIB),
        cost_estimate=pl.CostEstimate(
            flops=12 * HEADS * ROWS * PAIR_SPAN * HEAD_DIM,
            bytes_accessed=4 * MIB,
            transcendentals=HEADS * ROWS * PAIR_SPAN,
        ),
    )(queries, grads, *blocks)


def collect_kernel(own, swapped, near, far, grad_keys, grad_values):
    total = own[...].astype(jnp.float32) + swapped[0].astype(jnp.float32)
    total += near[...].astype(jnp.float32) + far[...].astype(jnp.float32)
    grad_keys[...] = total[:, :HEAD_DIM]
    grad_values[...] = total[:, HEAD_DIM:]


def collect(own, swapped, near, far):
    shape = jax.ShapeDtypeStruct((ROWS, HEAD_DIM), jnp.float32)
    return pl.pallas_call(
        collect_kernel,
        out_shape=(shape, shape),
        in_specs=[VMEM] * 4,
        out_specs=(VMEM, VMEM),
        cost_estimate=pl.CostEstimate(flops=MIB, bytes_accessed=MIB, transcendentals=0),
    )(own, swapped, near, far)


def at(half, chip, core):
    return half * 8 + (chip % CHIPS) * 2 + core


def per_device(queries, key_heads, value_heads, grad_output, token_logprob, doc_ids, response):
    spots = [(half, chip, core) for half in (0, 1) for chip in range(CHIPS) for core in (0, 1)]
    ahead = [(at(h, x, k), at(h, x + 1 - 2 * k, k)) for h, x, k in spots]
    cross = [(at(h, x, k), at(h, x + 1 - 2 * k, 1 - k)) for h, x, k in spots]
    back = [(there, here) for here, there in ahead]
    cross_back = [(there, here) for here, there in cross]
    swap = [(place, place ^ 1) for place in range(16)]

    def send(block, route):
        return lax.ppermute(block, "ka", route)

    own = pack(key_heads, value_heads, token_logprob, doc_ids, response)
    near = send(own, ahead)
    far = send(own, back)
    own_s = send(own, swap)
    opposite = send(near, ahead)
    opposite_s = send(near, cross)
    near_s = send(near, swap)
    far_s = send(far, swap)

    blocks = (own, near, far, opposite, own_s, near_s, far_s, opposite_s)
    attention, grad_queries, own_p, near_p, far_p, opposite_p, swap_p, opposite_s_p, margin = (
        attend(queries, grad_output, blocks)
    )
    passed = send(opposite_p, back)
    passed_s = send(opposite_s_p, cross_back)
    swapped = send(swap_p, swap)
    whole = range(256)
    margin = sum(
        (lax.ppermute(margin, ("pb", "ka"), [(p, p ^ bits) for p in whole]) for bits in (8, 16, 24)),
        margin,
    )
    wide = jnp.float32
    near_sum = (near_p.astype(wide) + swapped[1] + passed + passed_s).astype(jnp.bfloat16)
    far_sum = far_p + swapped[2]
    near_part = send(near_sum, back)
    far_part = send(far_sum, ahead)
    margin = sum(
        (lax.ppermute(margin, "pb", [(p, p ^ bits) for p in range(16)]) for bits in range(2, 16, 2)),
        margin,
    )
    grad_keys, grad_values = collect(own_p, swapped, near_part, far_part)
    return (attention, grad_queries, grad_keys, grad_values, margin[0, :PAIRS])


def solution(mesh):
    rows = P(("pb", "ka"), None)
    line = P(("pb", "ka"))
    return jax.shard_map(
        per_device,
        mesh=mesh,
        in_specs=(rows, rows, rows, rows, line, line, line),
        out_specs=(rows, rows, rows, rows, P()),
        check_vma=False,
    )
```

```python
import math

import jax
import jax.numpy as jnp
from jax import lax
from jax.experimental import pallas as pl
from jax.experimental.pallas import tpu as pltpu
from jax.sharding import PartitionSpec as P

HEAD_DIM = 128
HEADS = 6
PAIR_SPAN = 2048
ROWS = 256
BLOCKS = PAIR_SPAN // ROWS
CHIPS = 4
PAIRS = 32
PACKED = 2 * ROWS + 16
NEG = -1e30
INV_ROOT = 1.0 / math.sqrt(HEAD_DIM)
SCALE2 = INV_ROOT * math.log2(math.e)

VMEM = pl.BlockSpec(memory_space=pltpu.VMEM)
HBM = pl.BlockSpec(memory_space=pltpu.HBM)
MIB = 1024 * 1024


def dot(a, b):
    return jnp.dot(a, b, preferred_element_type=jnp.float32)


def split(value):
    high = value.astype(jnp.bfloat16).astype(jnp.float32)
    middle = (value - high).astype(jnp.bfloat16).astype(jnp.float32)
    return high, middle, value - high - middle


def pack_kernel(keys, values, logprob, docs, response, packed):
    odd = (docs[...] & 1).astype(jnp.float32)
    even = 1.0 - odd
    live = response[...].astype(jnp.float32)
    scored = logprob[...] * live
    first, second, first_live, second_live, count = (
        jnp.sum(term, keepdims=True)
        for term in (scored * even, scored * odd, live * even, live * odd, even)
    )
    terms = (*split(first), *split(second), first_live, second_live, count)
    lane = lax.broadcasted_iota(jnp.int32, (16, HEAD_DIM), 1)
    table = jnp.zeros((16, HEAD_DIM), jnp.float32)
    for place, term in enumerate(terms):
        table = jnp.where(lane == place, term, table)
    packed[:ROWS, :] = keys[...]
    packed[ROWS : 2 * ROWS, :] = values[...]
    packed[2 * ROWS :, :] = table.astype(jnp.bfloat16)


def pack(keys, values, logprob, docs, response):
    wide = (ROWS // 128, 128)
    return pl.pallas_call(
        pack_kernel,
        out_shape=jax.ShapeDtypeStruct((PACKED, HEAD_DIM), jnp.bfloat16),
        in_specs=[VMEM] * 5,
        out_specs=VMEM,
        cost_estimate=pl.CostEstimate(flops=10000, bytes_accessed=MIB // 2, transcendentals=0),
    )(keys, values, logprob.reshape(wide), docs.reshape(wide), response.reshape(wide))


def spans():
    return [(block, slice(block * ROWS, (block + 1) * ROWS)) for block in range(BLOCKS)]


def attend_kernel(
    queries_hbm, grads_hbm, own_hbm, near, far, opposite, own_s, near_s, far_s, opposite_s,
    attention, grad_queries, own_part, near_part, far_part, opposite_part, swap_parts,
    opposite_s_part,
    queries, grads, own, arrived, keys, values, keys_t, values_t, bias, scores, probs, grad_scores, acc_k, acc_v,
):
    fetches = [
        pltpu.make_async_copy(source, target, arrived.at[number])
        for number, (source, target) in enumerate(
            ((own_hbm, own), (queries_hbm, queries), (grads_hbm, grads))
        )
    ]
    for fetch in fetches:
        fetch.start()
    place = lax.axis_index("ka")
    core = lax.rem(place, 2)
    chip = lax.rem(place // 2, CHIPS)
    step = 1 - 2 * core
    chips = [chip, chip - step, chip + step, chip + 2, chip, chip + step, chip - step, chip + 2]
    first_row = lax.rem(place, BLOCKS) * ROWS
    blocks = (own, near, far, opposite, own_s, near_s, far_s, opposite_s)
    parts = (
        own_part, near_part, far_part, opposite_part,
        swap_parts.at[0], swap_parts.at[1], swap_parts.at[2], opposite_s_part,
    )
    totals = None
    for block, span in spans()[::-1]:
        if block == 0:
            fetches[0].wait()
        key = blocks[block][:ROWS, :]
        value = blocks[block][ROWS : 2 * ROWS, :]
        keys[span, :] = key
        values[span, :] = value
        keys_t[:, span] = key.T
        values_t[:, span] = value.T
        term = blocks[block][2 * ROWS :, :].astype(jnp.float32)
        totals = term if totals is None else totals + term
    totals = totals[:8, :]
    wide = lax.broadcasted_iota(jnp.int32, (8, HEAD_DIM), 1)
    cut = jnp.sum(jnp.where(wide == 8, totals, 0.0), axis=1, keepdims=True)[:1].astype(jnp.int32)
    row = first_row + lax.broadcasted_iota(jnp.int32, (ROWS, ROWS), 0)
    lane = lax.broadcasted_iota(jnp.int32, (ROWS, ROWS), 1)
    start = jnp.where(row >= cut, cut, 0)
    for block, span in spans():
        side = core if block < CHIPS else 1 - core
        col = lane + (lax.rem(chips[block] + CHIPS, CHIPS) * 2 + side) * ROWS
        bias[:, span] = jnp.where((col >= start) & (col <= row), 0.0, NEG)

    columns = [slice(head * HEAD_DIM, (head + 1) * HEAD_DIM) for head in range(HEADS)]

    def score_step(head, span, top):
        score = dot(queries[:, columns[head]], keys_t[:, span]) + bias[:, span]
        scores[head % 2, :, span] = score
        return score if top is None else jnp.maximum(top, score)

    def prob_step(head, span, row_max, total):
        prob = jnp.exp2(scores[head % 2, :, span] * SCALE2 - row_max)
        probs[head % 2, :, span] = prob.astype(jnp.bfloat16)
        return prob if total is None else total + prob

    def max_of(top):
        return jnp.max(top, axis=1, keepdims=True) * SCALE2

    fetches[1].wait()
    top = total = None
    for block, span in spans():
        top = score_step(0, span, top)
    row_max = max_of(top)
    for block, span in spans():
        total = prob_step(0, span, row_max, total)
    fetches[2].wait()
    for head in range(HEADS):
        slot = head % 2
        query = queries[:, columns[head]]
        inv_total = 1.0 / jnp.sum(total, axis=1, keepdims=True)
        output = (dot(probs[slot], values[...]) * inv_total).astype(jnp.bfloat16)
        attention[:, columns[head]] = output
        grad_wide = grads[:, columns[head]].astype(jnp.float32)
        delta = jnp.sum(grad_wide * output.astype(jnp.float32), axis=1, keepdims=True) * inv_total
        grad_scaled = (grad_wide * inv_total).astype(jnp.bfloat16)
        top = total = None
        for block, span in spans():
            grad_prob = dot(grad_scaled, values_t[:, span])
            if head < HEADS - 1:
                top = score_step(head + 1, span, top)
            grad_score = probs[slot, :, span].astype(jnp.float32) * (grad_prob - delta)
            grad_scores[slot, :, span] = grad_score.astype(jnp.bfloat16)
        if head < HEADS - 1:
            row_max = max_of(top)
        query_t = query.T
        grad_t = grad_scaled.T
        for block, span in spans():
            part_k = dot(query_t, grad_scores[slot, :, span])
            part_v = dot(grad_t, probs[slot, :, span])
            if head < HEADS - 1:
                total = prob_step(head + 1, span, row_max, total)
            if head:
                part_k += acc_k[:, span]
                part_v += acc_v[:, span]
            if head < HEADS - 1:
                acc_k[:, span] = part_k
                acc_v[:, span] = part_v
            else:
                parts[block][:, :HEAD_DIM] = (part_k * INV_ROOT).astype(jnp.bfloat16).T
                parts[block][:, HEAD_DIM:] = part_v.astype(jnp.bfloat16).T
        grad_queries[:, columns[head]] = dot(grad_scores[slot], keys[...]) * INV_ROOT


def attend(queries, grads, blocks):
    far_off = (queries, grads, blocks[0])
    width = HEADS * HEAD_DIM
    part = jax.ShapeDtypeStruct((ROWS, 2 * HEAD_DIM), jnp.bfloat16)
    return pl.pallas_call(
        attend_kernel,
        out_shape=(
            jax.ShapeDtypeStruct((ROWS, width), jnp.bfloat16),
            jax.ShapeDtypeStruct((ROWS, width), jnp.float32),
            part,
            part,
            part,
            part,
            jax.ShapeDtypeStruct((3, ROWS, 2 * HEAD_DIM), jnp.bfloat16),
            part,
        ),
        in_specs=[HBM] * 3 + [VMEM] * 7,
        out_specs=(VMEM,) * 8,
        scratch_shapes=[
            pltpu.VMEM((ROWS, width), jnp.bfloat16),
            pltpu.VMEM((ROWS, width), jnp.bfloat16),
            pltpu.VMEM((PACKED, HEAD_DIM), jnp.bfloat16),
            pltpu.SemaphoreType.DMA((3,)),
            pltpu.VMEM((PAIR_SPAN, HEAD_DIM), jnp.bfloat16),
            pltpu.VMEM((PAIR_SPAN, HEAD_DIM), jnp.bfloat16),
            pltpu.VMEM((HEAD_DIM, PAIR_SPAN), jnp.bfloat16),
            pltpu.VMEM((HEAD_DIM, PAIR_SPAN), jnp.bfloat16),
            pltpu.VMEM((ROWS, PAIR_SPAN), jnp.float32),
            pltpu.VMEM((2, ROWS, PAIR_SPAN), jnp.float32),
            pltpu.VMEM((2, ROWS, PAIR_SPAN), jnp.bfloat16),
            pltpu.VMEM((2, ROWS, PAIR_SPAN), jnp.bfloat16),
            pltpu.VMEM((HEAD_DIM, PAIR_SPAN), jnp.float32),
            pltpu.VMEM((HEAD_DIM, PAIR_SPAN), jnp.float32),
        ],
        compiler_params=pltpu.CompilerParams(vmem_limit_bytes=32 * MIB),
        cost_estimate=pl.CostEstimate(
            flops=12 * HEADS * ROWS * PAIR_SPAN * HEAD_DIM,
            bytes_accessed=4 * MIB,
            transcendentals=HEADS * ROWS * PAIR_SPAN,
        ),
    )(*(pltpu.with_memory_space_constraint(x, pltpu.HBM) for x in far_off), *blocks[1:])


def at(half, chip, core):
    return half * 8 + (chip % CHIPS) * 2 + core


def per_device(queries, key_heads, value_heads, grad_output, token_logprob, doc_ids, response):
    spots = [(half, chip, core) for half in (0, 1) for chip in range(CHIPS) for core in (0, 1)]
    ahead = [(at(h, x, k), at(h, x + 1 - 2 * k, k)) for h, x, k in spots]
    cross = [(at(h, x, k), at(h, x + 1 - 2 * k, 1 - k)) for h, x, k in spots]
    back = [(there, here) for here, there in ahead]
    cross_back = [(there, here) for here, there in cross]
    swap = [(place, place ^ 1) for place in range(16)]

    def send(block, route):
        return lax.ppermute(block, "ka", route)

    own = pack(key_heads, value_heads, token_logprob, doc_ids, response)
    near = send(own, ahead)
    far = send(own, back)
    own_s = send(own, swap)
    opposite = send(near, ahead)
    opposite_s = send(near, cross)
    near_s = send(near, swap)
    far_s = send(far, swap)

    blocks = (own, near, far, opposite, own_s, near_s, far_s, opposite_s)
    line = sum(block[2 * ROWS].astype(jnp.float32) for block in blocks)
    margin = (line[0] + line[1] + line[2]) / line[6] - (line[3] + line[4] + line[5]) / line[7]
    peers = [
        [(number // 2) * 16 + (number % 2) * BLOCKS + rank for number in range(PAIRS)]
        for rank in range(BLOCKS)
    ]
    margin, near = lax.optimization_barrier((jnp.broadcast_to(margin, (64, 128)), near))
    blocks = (own, near, *blocks[2:])
    margins = lax.all_gather(margin, ("pb", "ka"), axis_index_groups=peers)
    margins = lax.optimization_barrier(margins)
    attention, grad_queries, own_p, near_p, far_p, opposite_p, swap_p, opposite_s_p = attend(
        queries, grad_output, blocks
    )
    passed = send(opposite_p, back)
    passed_s = send(opposite_s_p, cross_back)
    swapped = send(swap_p, swap)
    wide = jnp.float32
    near_sum = (near_p.astype(wide) + swapped[1] + passed + passed_s).astype(jnp.bfloat16)
    far_sum = far_p + swapped[2]
    near_part = send(near_sum, back)
    far_part = send(far_sum, ahead)
    total = own_p.astype(wide) + swapped[0] + near_part + far_part
    return (attention, grad_queries, total[:, :HEAD_DIM], total[:, HEAD_DIM:], margins[:, 0, 0])


def solution(mesh):
    rows = P(("pb", "ka"), None)
    line = P(("pb", "ka"))
    return jax.shard_map(
        per_device,
        mesh=mesh,
        in_specs=(rows, rows, rows, rows, line, line, line),
        out_specs=(rows, rows, rows, rows, P()),
        check_vma=False,
    )
```

```python
import math

import jax
import jax.numpy as jnp
from jax import lax
from jax.experimental import pallas as pl
from jax.experimental.pallas import tpu as pltpu
from jax.sharding import PartitionSpec as P

HEAD_DIM = 128
HEADS = 6
PAIR_SPAN = 2048
ROWS = 256
BLOCKS = PAIR_SPAN // ROWS
CHIPS = 4
PAIRS = 32
PACKED = 2 * ROWS + 16
NEG = -1e30
INV_ROOT = 1.0 / math.sqrt(HEAD_DIM)
SCALE2 = INV_ROOT * math.log2(math.e)

VMEM = pl.BlockSpec(memory_space=pltpu.VMEM)
HBM = pl.BlockSpec(memory_space=pltpu.HBM)
MIB = 1024 * 1024


def dot(a, b):
    return jnp.dot(a, b, preferred_element_type=jnp.float32)


def split(value):
    high = value.astype(jnp.bfloat16).astype(jnp.float32)
    middle = (value - high).astype(jnp.bfloat16).astype(jnp.float32)
    return high, middle, value - high - middle


def pack_kernel(keys, values, logprob, docs, response, packed):
    odd = (docs[...] & 1).astype(jnp.float32)
    even = 1.0 - odd
    live = response[...].astype(jnp.float32)
    scored = logprob[...] * live
    first, second, first_live, second_live, count = (
        jnp.sum(term, keepdims=True)
        for term in (scored * even, scored * odd, live * even, live * odd, even)
    )
    terms = (*split(first), *split(second), first_live, second_live, count)
    lane = lax.broadcasted_iota(jnp.int32, (16, HEAD_DIM), 1)
    table = jnp.zeros((16, HEAD_DIM), jnp.float32)
    for place, term in enumerate(terms):
        table = jnp.where(lane == place, term, table)
    packed[:ROWS, :] = keys[...]
    packed[ROWS : 2 * ROWS, :] = values[...]
    packed[2 * ROWS :, :] = table.astype(jnp.bfloat16)


def pack(keys, values, logprob, docs, response):
    wide = (ROWS // 128, 128)
    return pl.pallas_call(
        pack_kernel,
        out_shape=jax.ShapeDtypeStruct((PACKED, HEAD_DIM), jnp.bfloat16),
        in_specs=[VMEM] * 5,
        out_specs=VMEM,
        cost_estimate=pl.CostEstimate(flops=10000, bytes_accessed=MIB // 2, transcendentals=0),
    )(keys, values, logprob.reshape(wide), docs.reshape(wide), response.reshape(wide))


def spans():
    return [(block, slice(block * ROWS, (block + 1) * ROWS)) for block in range(BLOCKS)]


def attend_kernel(
    queries_hbm, grads_hbm, own_hbm, near, far, opposite, own_s, near_s, far_s, opposite_s,
    attention, grad_queries, own_part, near_part, far_part, opposite_part, swap_parts,
    opposite_s_part, margin,
    queries, grads, own, arrived, keys, values, keys_t, values_t, bias, scores, probs, grad_scores, acc_k, acc_v,
):
    fetches = [
        pltpu.make_async_copy(source, target, arrived.at[number])
        for number, (source, target) in enumerate(
            ((own_hbm, own), (queries_hbm, queries), (grads_hbm, grads))
        )
    ]
    for fetch in fetches:
        fetch.start()
    place = lax.axis_index("ka")
    core = lax.rem(place, 2)
    chip = lax.rem(place // 2, CHIPS)
    step = 1 - 2 * core
    chips = [chip, chip - step, chip + step, chip + 2, chip, chip + step, chip - step, chip + 2]
    first_row = lax.rem(place, BLOCKS) * ROWS
    blocks = (own, near, far, opposite, own_s, near_s, far_s, opposite_s)
    parts = (
        own_part, near_part, far_part, opposite_part,
        swap_parts.at[0], swap_parts.at[1], swap_parts.at[2], opposite_s_part,
    )
    totals = None
    for block, span in spans()[::-1]:
        if block == 0:
            fetches[0].wait()
        key = blocks[block][:ROWS, :]
        value = blocks[block][ROWS : 2 * ROWS, :]
        keys[span, :] = key
        values[span, :] = value
        keys_t[:, span] = key.T
        values_t[:, span] = value.T
        term = blocks[block][2 * ROWS :, :].astype(jnp.float32)
        totals = term if totals is None else totals + term
    totals = totals[:8, :]
    wide = lax.broadcasted_iota(jnp.int32, (8, HEAD_DIM), 1)

    def total_of(low, high):
        chosen = jnp.where((wide >= low) & (wide < high), totals, 0.0)
        return jnp.sum(chosen, axis=1, keepdims=True)

    pair = lax.axis_index("pb") * 2 + place // BLOCKS
    value = total_of(0, 3) / total_of(6, 7) - total_of(3, 6) / total_of(7, 8)
    margin[...] = jnp.broadcast_to(jnp.where(wide == pair, value, 0.0)[None], margin.shape)
    cut = total_of(8, 9)[:1].astype(jnp.int32)
    row = first_row + lax.broadcasted_iota(jnp.int32, (ROWS, ROWS), 0)
    lane = lax.broadcasted_iota(jnp.int32, (ROWS, ROWS), 1)
    start = jnp.where(row >= cut, cut, 0)
    for block, span in spans():
        side = core if block < CHIPS else 1 - core
        col = lane + (lax.rem(chips[block] + CHIPS, CHIPS) * 2 + side) * ROWS
        bias[:, span] = jnp.where((col >= start) & (col <= row), 0.0, NEG)

    columns = [slice(head * HEAD_DIM, (head + 1) * HEAD_DIM) for head in range(HEADS)]

    def score_step(head, span, top):
        score = dot(queries[:, columns[head]], keys_t[:, span]) + bias[:, span]
        scores[head % 2, :, span] = score
        folded = jnp.maximum(score[:, :128], score[:, 128:])
        return folded if top is None else jnp.maximum(top, folded)

    def prob_step(head, span, row_max, total):
        prob = jnp.exp2(scores[head % 2, :, span] * SCALE2 - row_max)
        probs[head % 2, :, span] = prob.astype(jnp.bfloat16)
        folded = prob[:, :128] + prob[:, 128:]
        return folded if total is None else total + folded

    def max_of(top):
        return jnp.max(top, axis=1, keepdims=True) * SCALE2

    fetches[1].wait()
    top = total = None
    for block, span in spans():
        top = score_step(0, span, top)
    row_max = max_of(top)
    for block, span in spans():
        total = prob_step(0, span, row_max, total)
    fetches[2].wait()
    for head in range(HEADS):
        slot = head % 2
        query = queries[:, columns[head]]
        inv_total = 1.0 / jnp.sum(total, axis=1, keepdims=True)
        output = (dot(probs[slot], values[...]) * inv_total).astype(jnp.bfloat16)
        attention[:, columns[head]] = output
        grad_wide = grads[:, columns[head]].astype(jnp.float32)
        delta = jnp.sum(grad_wide * output.astype(jnp.float32), axis=1, keepdims=True) * inv_total
        grad_scaled = (grad_wide * inv_total).astype(jnp.bfloat16)
        top = total = None
        for block, span in spans():
            grad_prob = dot(grad_scaled, values_t[:, span])
            if head < HEADS - 1:
                top = score_step(head + 1, span, top)
            grad_score = probs[slot, :, span].astype(jnp.float32) * (grad_prob - delta)
            grad_scores[slot, :, span] = grad_score.astype(jnp.bfloat16)
        if head < HEADS - 1:
            row_max = max_of(top)
        query_t = query.T
        grad_t = grad_scaled.T
        for block, span in spans():
            part_k = dot(query_t, grad_scores[slot, :, span])
            part_v = dot(grad_t, probs[slot, :, span])
            if head < HEADS - 1:
                total = prob_step(head + 1, span, row_max, total)
            if head:
                part_k += acc_k[:, span]
                part_v += acc_v[:, span]
            if head < HEADS - 1:
                acc_k[:, span] = part_k
                acc_v[:, span] = part_v
            else:
                parts[block][:, :HEAD_DIM] = (part_k * INV_ROOT).astype(jnp.bfloat16).T
                parts[block][:, HEAD_DIM:] = part_v.astype(jnp.bfloat16).T
        grad_queries[:, columns[head]] = dot(grad_scores[slot], keys[...]) * INV_ROOT


def attend(queries, grads, blocks):
    far_off = (queries, grads, blocks[0])
    width = HEADS * HEAD_DIM
    part = jax.ShapeDtypeStruct((ROWS, 2 * HEAD_DIM), jnp.bfloat16)
    return pl.pallas_call(
        attend_kernel,
        out_shape=(
            jax.ShapeDtypeStruct((ROWS, width), jnp.bfloat16),
            jax.ShapeDtypeStruct((ROWS, width), jnp.float32),
            part,
            part,
            part,
            part,
            jax.ShapeDtypeStruct((3, ROWS, 2 * HEAD_DIM), jnp.bfloat16),
            part,
            jax.ShapeDtypeStruct((8, 8, HEAD_DIM), jnp.float32),
        ),
        in_specs=[HBM] * 3 + [VMEM] * 7,
        out_specs=(VMEM,) * 9,
        scratch_shapes=[
            pltpu.VMEM((ROWS, width), jnp.bfloat16),
            pltpu.VMEM((ROWS, width), jnp.bfloat16),
            pltpu.VMEM((PACKED, HEAD_DIM), jnp.bfloat16),
            pltpu.SemaphoreType.DMA((3,)),
            pltpu.VMEM((PAIR_SPAN, HEAD_DIM), jnp.bfloat16),
            pltpu.VMEM((PAIR_SPAN, HEAD_DIM), jnp.bfloat16),
            pltpu.VMEM((HEAD_DIM, PAIR_SPAN), jnp.bfloat16),
            pltpu.VMEM((HEAD_DIM, PAIR_SPAN), jnp.bfloat16),
            pltpu.VMEM((ROWS, PAIR_SPAN), jnp.float32),
            pltpu.VMEM((2, ROWS, PAIR_SPAN), jnp.float32),
            pltpu.VMEM((2, ROWS, PAIR_SPAN), jnp.bfloat16),
            pltpu.VMEM((2, ROWS, PAIR_SPAN), jnp.bfloat16),
            pltpu.VMEM((HEAD_DIM, PAIR_SPAN), jnp.float32),
            pltpu.VMEM((HEAD_DIM, PAIR_SPAN), jnp.float32),
        ],
        compiler_params=pltpu.CompilerParams(vmem_limit_bytes=32 * MIB),
        cost_estimate=pl.CostEstimate(
            flops=12 * HEADS * ROWS * PAIR_SPAN * HEAD_DIM,
            bytes_accessed=4 * MIB,
            transcendentals=HEADS * ROWS * PAIR_SPAN,
        ),
    )(*(pltpu.with_memory_space_constraint(x, pltpu.HBM) for x in far_off), *blocks[1:])


def at(half, chip, core):
    return half * 8 + (chip % CHIPS) * 2 + core


def per_device(queries, key_heads, value_heads, grad_output, token_logprob, doc_ids, response):
    spots = [(half, chip, core) for half in (0, 1) for chip in range(CHIPS) for core in (0, 1)]
    ahead = [(at(h, x, k), at(h, x + 1 - 2 * k, k)) for h, x, k in spots]
    cross = [(at(h, x, k), at(h, x + 1 - 2 * k, 1 - k)) for h, x, k in spots]
    back = [(there, here) for here, there in ahead]
    cross_back = [(there, here) for here, there in cross]
    swap = [(place, place ^ 1) for place in range(16)]

    def send(block, route):
        return lax.ppermute(block, "ka", route)

    own = pack(key_heads, value_heads, token_logprob, doc_ids, response)
    near = send(own, ahead)
    far = send(own, back)
    own_s = send(own, swap)
    opposite = send(near, ahead)
    opposite_s = send(near, cross)
    near_s = send(near, swap)
    far_s = send(far, swap)

    blocks = (own, near, far, opposite, own_s, near_s, far_s, opposite_s)
    attention, grad_queries, own_p, near_p, far_p, opposite_p, swap_p, opposite_s_p, margin = (
        attend(queries, grad_output, blocks)
    )
    passed = send(opposite_p, back)
    passed_s = send(opposite_s_p, cross_back)
    swapped = send(swap_p, swap)
    swapped, margin = lax.optimization_barrier((swapped, margin))
    columns = [list(range(low, 16, 2)) for low in (0, 1)]
    margin = jnp.sum(lax.all_to_all(margin, "pb", 0, 0, axis_index_groups=columns, tiled=True), axis=0)
    passed, margin = lax.optimization_barrier((passed, margin))
    wide = jnp.float32
    near_sum = (near_p.astype(wide) + swapped[1] + passed + passed_s).astype(jnp.bfloat16)
    far_sum = far_p + swapped[2]
    near_part = send(near_sum, back)
    far_part = send(far_sum, ahead)
    far_part, margin = lax.optimization_barrier((far_part, margin))
    turns = [[(place, place ^ bits) for place in range(256)] for bits in (8, 16, 24)]
    margin = sum((lax.ppermute(margin, ("pb", "ka"), turn) for turn in turns), margin)
    total = own_p.astype(wide) + swapped[0] + near_part + far_part
    return (attention, grad_queries, total[:, :HEAD_DIM], total[:, HEAD_DIM:], margin[0, :PAIRS])


def solution(mesh):
    rows = P(("pb", "ka"), None)
    line = P(("pb", "ka"))
    return jax.shard_map(
        per_device,
        mesh=mesh,
        in_specs=(rows, rows, rows, rows, line, line, line),
        out_specs=(rows, rows, rows, rows, P()),
        check_vma=False,
    )
```

```python
import math

import jax
import jax.numpy as jnp
from jax import lax
from jax.experimental import pallas as pl
from jax.experimental.pallas import tpu as pltpu
from jax.sharding import PartitionSpec as P

HEAD_DIM = 128
HEADS = 6
PAIR_SPAN = 2048
ROWS = 256
BLOCKS = PAIR_SPAN // ROWS
CHIPS = 4
PAIRS = 32
PACKED = 2 * ROWS + 16
NEG = -1e30
INV_ROOT = 1.0 / math.sqrt(HEAD_DIM)
SCALE2 = INV_ROOT * math.log2(math.e)

VMEM = pl.BlockSpec(memory_space=pltpu.VMEM)
HBM = pl.BlockSpec(memory_space=pltpu.HBM)
MIB = 1024 * 1024


def dot(a, b):
    return jnp.dot(a, b, preferred_element_type=jnp.float32)


def split(value):
    high = value.astype(jnp.bfloat16).astype(jnp.float32)
    middle = (value - high).astype(jnp.bfloat16).astype(jnp.float32)
    return high, middle, value - high - middle


def pack_kernel(keys, values, logprob, docs, response, packed):
    odd = (docs[...] & 1).astype(jnp.float32)
    even = 1.0 - odd
    live = response[...].astype(jnp.float32)
    scored = logprob[...] * live
    first, second, first_live, second_live, count = (
        jnp.sum(term, keepdims=True)
        for term in (scored * even, scored * odd, live * even, live * odd, even)
    )
    terms = (*split(first), *split(second), first_live, second_live, count)
    lane = lax.broadcasted_iota(jnp.int32, (16, HEAD_DIM), 1)
    table = jnp.zeros((16, HEAD_DIM), jnp.float32)
    for place, term in enumerate(terms):
        table = jnp.where(lane == place, term, table)
    packed[:ROWS, :] = keys[...]
    packed[ROWS : 2 * ROWS, :] = values[...]
    packed[2 * ROWS :, :] = table.astype(jnp.bfloat16)


def pack(keys, values, logprob, docs, response):
    wide = (ROWS // 128, 128)
    return pl.pallas_call(
        pack_kernel,
        out_shape=pltpu.VMEM((PACKED, HEAD_DIM), jnp.bfloat16),
        in_specs=[VMEM] * 5,
        out_specs=VMEM,
        cost_estimate=pl.CostEstimate(flops=10000, bytes_accessed=MIB // 2, transcendentals=0),
    )(keys, values, logprob.reshape(wide), docs.reshape(wide), response.reshape(wide))


def spans():
    return [(block, slice(block * ROWS, (block + 1) * ROWS)) for block in range(BLOCKS)]


def attend_kernel(
    queries_hbm, grads_hbm, own, near, far, opposite, own_s, near_s, far_s, opposite_s,
    attention_hbm, grad_queries_hbm, own_part, near_part, far_part, opposite_part, swap_parts,
    opposite_s_part, margin,
    queries, grads, attention, grad_queries, arrived, left, keys, values, keys_t, values_t, bias, scores, probs, grad_scores, acc_k, acc_v,
):
    fetches = [
        pltpu.make_async_copy(source, target, arrived.at[number])
        for number, (source, target) in enumerate(
            ((queries_hbm, queries), (grads_hbm, grads))
        )
    ]
    for fetch in fetches:
        fetch.start()
    place = lax.axis_index("ka")
    core = lax.rem(place, 2)
    chip = lax.rem(place // 2, CHIPS)
    step = 1 - 2 * core
    chips = [chip, chip - step, chip + step, chip + 2, chip, chip + step, chip - step, chip + 2]
    first_row = lax.rem(place, BLOCKS) * ROWS
    blocks = (own, near, far, opposite, own_s, near_s, far_s, opposite_s)
    parts = (
        own_part, near_part, far_part, opposite_part,
        swap_parts.at[0], swap_parts.at[1], swap_parts.at[2], opposite_s_part,
    )
    totals = None
    for block, span in spans():
        key = blocks[block][:ROWS, :]
        value = blocks[block][ROWS : 2 * ROWS, :]
        keys[span, :] = key
        values[span, :] = value
        keys_t[:, span] = key.T
        values_t[:, span] = value.T
        term = blocks[block][2 * ROWS :, :].astype(jnp.float32)
        totals = term if totals is None else totals + term
    totals = totals[:8, :]
    wide = lax.broadcasted_iota(jnp.int32, (8, HEAD_DIM), 1)

    def total_of(low, high):
        chosen = jnp.where((wide >= low) & (wide < high), totals, 0.0)
        return jnp.sum(chosen, axis=1, keepdims=True)

    pair = lax.axis_index("pb") * 2 + place // BLOCKS
    value = total_of(0, 3) / total_of(6, 7) - total_of(3, 6) / total_of(7, 8)
    margin[...] = jnp.broadcast_to(jnp.where(wide == pair, value, 0.0)[None], margin.shape)
    cut = total_of(8, 9)[:1].astype(jnp.int32)
    row = first_row + lax.broadcasted_iota(jnp.int32, (ROWS, ROWS), 0)
    lane = lax.broadcasted_iota(jnp.int32, (ROWS, ROWS), 1)
    start = jnp.where(row >= cut, cut, 0)
    for block, span in spans():
        side = core if block < CHIPS else 1 - core
        col = lane + (lax.rem(chips[block] + CHIPS, CHIPS) * 2 + side) * ROWS
        bias[:, span] = jnp.where((col >= start) & (col <= row), 0.0, NEG)

    columns = [slice(head * HEAD_DIM, (head + 1) * HEAD_DIM) for head in range(HEADS)]

    def score_step(head, span, top):
        score = dot(queries[:, columns[head]], keys_t[:, span]) + bias[:, span]
        scores[head % 2, :, span] = score
        folded = jnp.maximum(score[:, :128], score[:, 128:])
        return folded if top is None else jnp.maximum(top, folded)

    def prob_step(head, span, row_max, total):
        prob = jnp.exp2(scores[head % 2, :, span] * SCALE2 - row_max)
        probs[head % 2, :, span] = prob.astype(jnp.bfloat16)
        folded = prob[:, :128] + prob[:, 128:]
        return folded if total is None else total + folded

    def max_of(top):
        return jnp.max(top, axis=1, keepdims=True) * SCALE2

    fetches[0].wait()
    top = total = None
    for block, span in spans():
        top = score_step(0, span, top)
    row_max = max_of(top)
    for block, span in spans():
        total = prob_step(0, span, row_max, total)
    fetches[1].wait()
    writes = []
    for head in range(HEADS):
        slot = head % 2
        query = queries[:, columns[head]]
        inv_total = 1.0 / jnp.sum(total, axis=1, keepdims=True)
        output = (dot(probs[slot], values[...]) * inv_total).astype(jnp.bfloat16)
        attention[:, columns[head]] = output
        grad_wide = grads[:, columns[head]].astype(jnp.float32)
        delta = jnp.sum(grad_wide * output.astype(jnp.float32), axis=1, keepdims=True) * inv_total
        grad_scaled = (grad_wide * inv_total).astype(jnp.bfloat16)
        top = total = None
        for block, span in spans():
            grad_prob = dot(grad_scaled, values_t[:, span])
            if head < HEADS - 1:
                top = score_step(head + 1, span, top)
            grad_score = probs[slot, :, span].astype(jnp.float32) * (grad_prob - delta)
            grad_scores[slot, :, span] = grad_score.astype(jnp.bfloat16)
        if head < HEADS - 1:
            row_max = max_of(top)
        grad_queries[:, columns[head]] = dot(grad_scores[slot], keys[...]) * INV_ROOT
        for kind, (source, target) in enumerate(
            ((attention, attention_hbm), (grad_queries, grad_queries_hbm))
        ):
            write = pltpu.make_async_copy(
                source.at[:, columns[head]], target.at[:, columns[head]], left.at[2 * head + kind]
            )
            write.start()
            writes.append(write)
        query_t = query.T
        grad_t = grad_scaled.T
        for block, span in spans():
            part_k = dot(query_t, grad_scores[slot, :, span])
            part_v = dot(grad_t, probs[slot, :, span])
            if head < HEADS - 1:
                total = prob_step(head + 1, span, row_max, total)
            if head:
                part_k += acc_k[:, span]
                part_v += acc_v[:, span]
            if head < HEADS - 1:
                acc_k[:, span] = part_k
                acc_v[:, span] = part_v
            else:
                parts[block][:, :HEAD_DIM] = (part_k * INV_ROOT).astype(jnp.bfloat16).T
                parts[block][:, HEAD_DIM:] = part_v.astype(jnp.bfloat16).T
    for write in writes:
        write.wait()


def attend(queries, grads, blocks):
    width = HEADS * HEAD_DIM
    part = jax.ShapeDtypeStruct((ROWS, 2 * HEAD_DIM), jnp.bfloat16)
    return pl.pallas_call(
        attend_kernel,
        out_shape=(
            jax.ShapeDtypeStruct((ROWS, width), jnp.bfloat16),
            jax.ShapeDtypeStruct((ROWS, width), jnp.float32),
            part,
            part,
            part,
            part,
            jax.ShapeDtypeStruct((3, ROWS, 2 * HEAD_DIM), jnp.bfloat16),
            part,
            jax.ShapeDtypeStruct((8, 8, HEAD_DIM), jnp.float32),
        ),
        in_specs=[HBM] * 2 + [VMEM] * BLOCKS,
        out_specs=(HBM,) * 2 + (VMEM,) * 7,
        scratch_shapes=[
            pltpu.VMEM((ROWS, width), jnp.bfloat16),
            pltpu.VMEM((ROWS, width), jnp.bfloat16),
            pltpu.VMEM((ROWS, width), jnp.bfloat16),
            pltpu.VMEM((ROWS, width), jnp.float32),
            pltpu.SemaphoreType.DMA((2,)),
            pltpu.SemaphoreType.DMA((2 * HEADS,)),
            pltpu.VMEM((PAIR_SPAN, HEAD_DIM), jnp.bfloat16),
            pltpu.VMEM((PAIR_SPAN, HEAD_DIM), jnp.bfloat16),
            pltpu.VMEM((HEAD_DIM, PAIR_SPAN), jnp.bfloat16),
            pltpu.VMEM((HEAD_DIM, PAIR_SPAN), jnp.bfloat16),
            pltpu.VMEM((ROWS, PAIR_SPAN), jnp.float32),
            pltpu.VMEM((2, ROWS, PAIR_SPAN), jnp.float32),
            pltpu.VMEM((2, ROWS, PAIR_SPAN), jnp.bfloat16),
            pltpu.VMEM((2, ROWS, PAIR_SPAN), jnp.bfloat16),
            pltpu.VMEM((HEAD_DIM, PAIR_SPAN), jnp.float32),
            pltpu.VMEM((HEAD_DIM, PAIR_SPAN), jnp.float32),
        ],
        compiler_params=pltpu.CompilerParams(vmem_limit_bytes=32 * MIB),
        cost_estimate=pl.CostEstimate(
            flops=12 * HEADS * ROWS * PAIR_SPAN * HEAD_DIM,
            bytes_accessed=4 * MIB,
            transcendentals=HEADS * ROWS * PAIR_SPAN,
        ),
    )(*(pltpu.with_memory_space_constraint(x, pltpu.HBM) for x in (queries, grads)), *blocks)


def at(half, chip, core):
    return half * 8 + (chip % CHIPS) * 2 + core


def per_device(queries, key_heads, value_heads, grad_output, token_logprob, doc_ids, response):
    spots = [(half, chip, core) for half in (0, 1) for chip in range(CHIPS) for core in (0, 1)]
    ahead = [(at(h, x, k), at(h, x + 1 - 2 * k, k)) for h, x, k in spots]
    cross = [(at(h, x, k), at(h, x + 1 - 2 * k, 1 - k)) for h, x, k in spots]
    back = [(there, here) for here, there in ahead]
    cross_back = [(there, here) for here, there in cross]
    swap = [(place, place ^ 1) for place in range(16)]

    def send(block, route):
        return lax.ppermute(block, "ka", route)

    own = pack(key_heads, value_heads, token_logprob, doc_ids, response)
    near = send(own, ahead)
    far = send(own, back)
    own_s = send(own, swap)
    opposite = send(near, ahead)
    opposite_s = send(near, cross)
    near_s = send(near, swap)
    far_s = send(far, swap)

    blocks = (own, near, far, opposite, own_s, near_s, far_s, opposite_s)
    attention, grad_queries, own_p, near_p, far_p, opposite_p, swap_p, opposite_s_p, margin = (
        attend(queries, grad_output, blocks)
    )
    passed = send(opposite_p, back)
    passed_s = send(opposite_s_p, cross_back)
    swapped = send(swap_p, swap)
    swapped, margin = lax.optimization_barrier((swapped, margin))
    columns = [list(range(low, 16, 2)) for low in (0, 1)]
    margin = jnp.sum(lax.all_to_all(margin, "pb", 0, 0, axis_index_groups=columns, tiled=True), axis=0)
    passed, margin = lax.optimization_barrier((passed, margin))
    wide = jnp.float32
    near_sum = (near_p.astype(wide) + swapped[1] + passed + passed_s).astype(jnp.bfloat16)
    far_sum = far_p + swapped[2]
    near_part = send(near_sum, back)
    far_part = send(far_sum, ahead)
    _, far_part, margin = lax.optimization_barrier((near_sum, far_part, margin))
    turns = [[(place, place ^ bits) for place in range(256)] for bits in (8, 16, 24)]
    margin = sum((lax.ppermute(margin, ("pb", "ka"), turn) for turn in turns), margin)
    total = own_p.astype(wide) + swapped[0] + near_part + far_part
    return (attention, grad_queries, total[:, :HEAD_DIM], total[:, HEAD_DIM:], margin[0, :PAIRS])


def solution(mesh):
    rows = P(("pb", "ka"), None)
    line = P(("pb", "ka"))
    return jax.shard_map(
        per_device,
        mesh=mesh,
        in_specs=(rows, rows, rows, rows, line, line, line),
        out_specs=(rows, rows, rows, rows, P()),
        check_vma=False,
    )
```

```python
import math

import jax
import jax.numpy as jnp
from jax import lax
from jax.experimental import pallas as pl
from jax.experimental.pallas import tpu as pltpu
from jax.sharding import PartitionSpec as P

HEAD_DIM = 128
HEADS = 6
PAIR_SPAN = 2048
ROWS = 256
BLOCKS = PAIR_SPAN // ROWS
CHIPS = 4
PAIRS = 32
PACKED = 2 * ROWS + 16
EXTRA = 16
LIMBS = tuple(2.0 ** (6 - 5 * place) for place in range(6))
NEG = -1e30
INV_ROOT = 1.0 / math.sqrt(HEAD_DIM)
SCALE2 = INV_ROOT * math.log2(math.e)

VMEM = pl.BlockSpec(memory_space=pltpu.VMEM)
HBM = pl.BlockSpec(memory_space=pltpu.HBM)
MIB = 1024 * 1024


def dot(a, b):
    return jnp.dot(a, b, preferred_element_type=jnp.float32)


def pack_kernel(
    keys, values, logprob, docs, response, queries_hbm, grads_hbm,
    packed, sums, queries, grads, arrived,
):
    fetches = [
        pltpu.make_async_copy(source, target, arrived.at[number])
        for number, (source, target) in enumerate(((queries_hbm, queries), (grads_hbm, grads)))
    ]
    for fetch in fetches:
        fetch.start()
    pair = lax.axis_index("pb") * 2 + lax.axis_index("ka") // BLOCKS
    odd = (docs[...] & 1).astype(jnp.float32)
    even = 1.0 - odd
    live = response[...].astype(jnp.float32)
    scored = logprob[...] * live
    lane = lax.broadcasted_iota(jnp.int32, (8, HEAD_DIM), 1)
    table = jnp.zeros((8, HEAD_DIM), jnp.float32)
    for kind, term in enumerate((scored * even, scored * odd, live * even, live * odd)):
        table = jnp.where(lane == kind * PAIRS + pair, jnp.sum(term, keepdims=True), table)
    sums[...] = table
    packed[:ROWS, :] = keys[...]
    packed[ROWS : 2 * ROWS, :] = values[...]
    count = jnp.broadcast_to(jnp.sum(even, keepdims=True), (16, HEAD_DIM))
    packed[2 * ROWS :, :] = count.astype(jnp.bfloat16)
    for fetch in fetches:
        fetch.wait()


def pack(keys, values, logprob, docs, response, queries, grads):
    wide = (ROWS // 128, 128)
    far_off = (pltpu.with_memory_space_constraint(x, pltpu.HBM) for x in (queries, grads))
    return pl.pallas_call(
        pack_kernel,
        out_shape=(
            pltpu.VMEM((PACKED, HEAD_DIM), jnp.bfloat16),
            pltpu.VMEM((8, HEAD_DIM), jnp.float32),
            pltpu.VMEM(queries.shape, jnp.bfloat16),
            pltpu.VMEM(grads.shape, jnp.bfloat16),
        ),
        in_specs=[VMEM] * 5 + [HBM] * 2,
        out_specs=(VMEM,) * 4,
        scratch_shapes=[pltpu.SemaphoreType.DMA((2,))],
        cost_estimate=pl.CostEstimate(flops=10000, bytes_accessed=2 * MIB, transcendentals=0),
    )(keys, values, logprob.reshape(wide), docs.reshape(wide), response.reshape(wide), *far_off)


def spans():
    return [(block, slice(block * ROWS, (block + 1) * ROWS)) for block in range(BLOCKS)]


def attend_kernel(
    queries, grads, table, own, near, far, opposite, own_s, near_s, far_s, opposite_s,
    attention, grad_queries, own_part, near_part, far_part, opposite_part, swap_parts,
    opposite_s_part,
    keys, values, keys_t, values_t, bias, scores, probs, grad_scores, acc_k, acc_v,
):
    place = lax.axis_index("ka")
    core = lax.rem(place, 2)
    chip = lax.rem(place // 2, CHIPS)
    step = 1 - 2 * core
    chips = [chip, chip - step, chip + step, chip + 2, chip, chip + step, chip - step, chip + 2]
    first_row = lax.rem(place, BLOCKS) * ROWS
    blocks = (own, near, far, opposite, own_s, near_s, far_s, opposite_s)
    parts = (
        own_part, near_part, far_part, opposite_part,
        swap_parts.at[0], swap_parts.at[1], swap_parts.at[2], opposite_s_part,
    )
    count = None
    for block, span in spans():
        key = blocks[block][:ROWS, :]
        value = blocks[block][ROWS : 2 * ROWS, :]
        keys[span, :] = key
        values[span, :] = value
        keys_t[:, span] = key.T
        values_t[:, span] = value.T
        term = blocks[block][2 * ROWS :, :].astype(jnp.float32)
        count = term if count is None else count + term
    cut = count[:1, :1].astype(jnp.int32)
    rest = jnp.abs(table[:1, :])
    place_row = lax.broadcasted_iota(jnp.int32, (EXTRA, HEAD_DIM), 0)
    limbs = jnp.zeros((EXTRA, HEAD_DIM), jnp.float32)
    for number, scale in enumerate(LIMBS):
        limb = jnp.floor(rest * (1.0 / scale))
        rest = rest - limb * scale
        limbs = jnp.where(place_row == number, limb, limbs)
    limbs = limbs.astype(jnp.bfloat16)
    for part in parts:
        part[ROWS:, :HEAD_DIM] = limbs
        part[ROWS:, HEAD_DIM:] = limbs
    row = first_row + lax.broadcasted_iota(jnp.int32, (ROWS, ROWS), 0)
    lane = lax.broadcasted_iota(jnp.int32, (ROWS, ROWS), 1)
    start = jnp.where(row >= cut, cut, 0)
    for block, span in spans():
        side = core if block < CHIPS else 1 - core
        col = lane + (lax.rem(chips[block] + CHIPS, CHIPS) * 2 + side) * ROWS
        bias[:, span] = jnp.where((col >= start) & (col <= row), 0.0, NEG)

    columns = [slice(head * HEAD_DIM, (head + 1) * HEAD_DIM) for head in range(HEADS)]

    def score_step(head, span, top):
        score = dot(queries[:, columns[head]], keys_t[:, span]) + bias[:, span]
        scores[head % 2, :, span] = score
        folded = jnp.maximum(score[:, :128], score[:, 128:])
        return folded if top is None else jnp.maximum(top, folded)

    def prob_step(head, span, row_max, total):
        prob = jnp.exp2(scores[head % 2, :, span] * SCALE2 - row_max)
        probs[head % 2, :, span] = prob.astype(jnp.bfloat16)
        folded = prob[:, :128] + prob[:, 128:]
        return folded if total is None else total + folded

    def max_of(top):
        return jnp.max(top, axis=1, keepdims=True) * SCALE2

    top = total = None
    for block, span in spans():
        top = score_step(0, span, top)
    row_max = max_of(top)
    for block, span in spans():
        total = prob_step(0, span, row_max, total)
    for head in range(HEADS):
        slot = head % 2
        query = queries[:, columns[head]]
        inv_total = 1.0 / jnp.sum(total, axis=1, keepdims=True)
        output = (dot(probs[slot], values[...]) * inv_total).astype(jnp.bfloat16)
        attention[:, columns[head]] = output
        grad_wide = grads[:, columns[head]].astype(jnp.float32)
        delta = jnp.sum(grad_wide * output.astype(jnp.float32), axis=1, keepdims=True) * inv_total
        grad_scaled = (grad_wide * inv_total).astype(jnp.bfloat16)
        top = total = None
        for block, span in spans():
            grad_prob = dot(grad_scaled, values_t[:, span])
            if head < HEADS - 1:
                top = score_step(head + 1, span, top)
            grad_score = probs[slot, :, span].astype(jnp.float32) * (grad_prob - delta)
            grad_scores[slot, :, span] = grad_score.astype(jnp.bfloat16)
        if head < HEADS - 1:
            row_max = max_of(top)
        query_t = query.T
        grad_t = grad_scaled.T
        for block, span in spans():
            part_k = dot(query_t, grad_scores[slot, :, span])
            part_v = dot(grad_t, probs[slot, :, span])
            if head < HEADS - 1:
                total = prob_step(head + 1, span, row_max, total)
            if head:
                part_k += acc_k[:, span]
                part_v += acc_v[:, span]
            if head < HEADS - 1:
                acc_k[:, span] = part_k
                acc_v[:, span] = part_v
            else:
                parts[block][:ROWS, :HEAD_DIM] = (part_k * INV_ROOT).astype(jnp.bfloat16).T
                parts[block][:ROWS, HEAD_DIM:] = part_v.astype(jnp.bfloat16).T
        grad_queries[:, columns[head]] = dot(grad_scores[slot], keys[...]) * INV_ROOT


def attend(queries, grads, table, blocks):
    width = HEADS * HEAD_DIM
    part = jax.ShapeDtypeStruct((ROWS + EXTRA, 2 * HEAD_DIM), jnp.bfloat16)
    return pl.pallas_call(
        attend_kernel,
        out_shape=(
            jax.ShapeDtypeStruct((ROWS, width), jnp.bfloat16),
            jax.ShapeDtypeStruct((ROWS, width), jnp.float32),
            part,
            part,
            part,
            part,
            jax.ShapeDtypeStruct((3, ROWS + EXTRA, 2 * HEAD_DIM), jnp.bfloat16),
            part,
        ),
        in_specs=[VMEM] * (3 + BLOCKS),
        out_specs=(VMEM,) * 8,
        scratch_shapes=[
            pltpu.VMEM((PAIR_SPAN, HEAD_DIM), jnp.bfloat16),
            pltpu.VMEM((PAIR_SPAN, HEAD_DIM), jnp.bfloat16),
            pltpu.VMEM((HEAD_DIM, PAIR_SPAN), jnp.bfloat16),
            pltpu.VMEM((HEAD_DIM, PAIR_SPAN), jnp.bfloat16),
            pltpu.VMEM((ROWS, PAIR_SPAN), jnp.float32),
            pltpu.VMEM((2, ROWS, PAIR_SPAN), jnp.float32),
            pltpu.VMEM((2, ROWS, PAIR_SPAN), jnp.bfloat16),
            pltpu.VMEM((2, ROWS, PAIR_SPAN), jnp.bfloat16),
            pltpu.VMEM((HEAD_DIM, PAIR_SPAN), jnp.float32),
            pltpu.VMEM((HEAD_DIM, PAIR_SPAN), jnp.float32),
        ],
        compiler_params=pltpu.CompilerParams(vmem_limit_bytes=32 * MIB),
        cost_estimate=pl.CostEstimate(
            flops=12 * HEADS * ROWS * PAIR_SPAN * HEAD_DIM,
            bytes_accessed=4 * MIB,
            transcendentals=HEADS * ROWS * PAIR_SPAN,
        ),
    )(queries, grads, table, *blocks)


def at(half, chip, core):
    return half * 8 + (chip % CHIPS) * 2 + core


def per_device(queries, key_heads, value_heads, grad_output, token_logprob, doc_ids, response):
    spots = [(half, chip, core) for half in (0, 1) for chip in range(CHIPS) for core in (0, 1)]
    ahead = [(at(h, x, k), at(h, x + 1 - 2 * k, k)) for h, x, k in spots]
    cross = [(at(h, x, k), at(h, x + 1 - 2 * k, 1 - k)) for h, x, k in spots]
    back = [(there, here) for here, there in ahead]
    cross_back = [(there, here) for here, there in cross]
    swap = [(place, place ^ 1) for place in range(16)]

    def send(block, route):
        return lax.ppermute(block, "ka", route)

    def exchange(table, axis, masks):
        extent = range(lax.axis_size(axis))
        routes = [[(place, place ^ mask) for place in extent] for mask in masks]
        return sum((lax.ppermute(table, axis, route) for route in routes), table)

    own, table, queries, grad_output = pack(
        key_heads, value_heads, token_logprob, doc_ids, response, queries, grad_output
    )
    near = send(own, ahead)
    far = send(own, back)
    own_s = send(own, swap)
    own_s, table = lax.optimization_barrier((own_s, table))
    table = exchange(table, "pb", (4, 8, 12))
    table = exchange(table, "ka", (8,))
    opposite = send(near, ahead)
    opposite_s = send(near, cross)
    near_s = send(near, swap)
    far_s = send(far, swap)
    near_s, table = lax.optimization_barrier((near_s, table))
    table = exchange(table, "pb", (1, 2, 3))

    blocks = (own, near, far, opposite, own_s, near_s, far_s, opposite_s)
    attention, grad_queries, own_p, near_p, far_p, opposite_p, swap_p, opposite_s_p = attend(
        queries, grad_output, table, blocks
    )
    passed = send(opposite_p, back)
    passed_s = send(opposite_s_p, cross_back)
    swapped = send(swap_p, swap)
    wide = jnp.float32
    near_sum = (near_p.astype(wide) + swapped[1] + passed + passed_s).astype(jnp.bfloat16)
    far_sum = far_p + swapped[2]
    near_part = send(near_sum, back)
    far_part = send(far_sum, ahead)
    total = own_p.astype(wide) + swapped[0] + near_part + far_part
    grad_keys, grad_values = total[:ROWS, :HEAD_DIM], total[:ROWS, HEAD_DIM:]
    sums = sum(total[ROWS + number, :HEAD_DIM] * scale for number, scale in enumerate(LIMBS))
    sums = sums.reshape(4, PAIRS)
    margins = sums[1] / sums[3] - sums[0] / sums[2]
    return (attention, grad_queries, grad_keys, grad_values, margins)


def solution(mesh):
    rows = P(("pb", "ka"), None)
    line = P(("pb", "ka"))
    return jax.shard_map(
        per_device,
        mesh=mesh,
        in_specs=(rows, rows, rows, rows, line, line, line),
        out_specs=(rows, rows, rows, rows, P()),
        check_vma=False,
    )
```

```python
import math

import jax
import jax.numpy as jnp
from jax import lax
from jax.experimental import pallas as pl
from jax.experimental.pallas import tpu as pltpu
from jax.sharding import PartitionSpec as P

HEAD_DIM = 128
HEADS = 6
PAIR_SPAN = 2048
ROWS = 256
BLOCKS = PAIR_SPAN // ROWS
CHIPS = 4
PAIRS = 32
PACKED = 2 * ROWS + 16
NEG = -1e30
INV_ROOT = 1.0 / math.sqrt(HEAD_DIM)
SCALE2 = INV_ROOT * math.log2(math.e)

VMEM = pl.BlockSpec(memory_space=pltpu.VMEM)
HBM = pl.BlockSpec(memory_space=pltpu.HBM)
MIB = 1024 * 1024


def dot(a, b):
    return jnp.dot(a, b, preferred_element_type=jnp.float32)


def fetch_kernel(queries_hbm, grads_hbm, queries, grads, arrived):
    fetches = [
        pltpu.make_async_copy(source, target, arrived.at[number])
        for number, (source, target) in enumerate(((queries_hbm, queries), (grads_hbm, grads)))
    ]
    for fetch in fetches:
        fetch.start()
    for fetch in fetches:
        fetch.wait()


def fetch(queries, grads):
    return pl.pallas_call(
        fetch_kernel,
        out_shape=(
            pltpu.VMEM(queries.shape, jnp.bfloat16),
            pltpu.VMEM(grads.shape, jnp.bfloat16),
        ),
        in_specs=[HBM] * 2,
        out_specs=(VMEM,) * 2,
        scratch_shapes=[pltpu.SemaphoreType.DMA((2,))],
        cost_estimate=pl.CostEstimate(flops=0, bytes_accessed=2 * MIB, transcendentals=0),
    )(*(pltpu.with_memory_space_constraint(x, pltpu.HBM) for x in (queries, grads)))


def pack_kernel(keys, values, logprob, docs, response, packed, sums):
    pair = lax.axis_index("pb") * 2 + lax.axis_index("ka") // BLOCKS
    odd = (docs[...] & 1).astype(jnp.float32)
    even = 1.0 - odd
    live = response[...].astype(jnp.float32)
    scored = logprob[...] * live
    lane = lax.broadcasted_iota(jnp.int32, (8, HEAD_DIM), 1)
    table = jnp.zeros((8, HEAD_DIM), jnp.float32)
    for kind, term in enumerate((scored * even, scored * odd, live * even, live * odd)):
        table = jnp.where(lane == kind * PAIRS + pair, jnp.sum(term, keepdims=True), table)
    sums[...] = jnp.broadcast_to(table[:1], sums.shape)
    packed[:ROWS, :] = keys[...]
    packed[ROWS : 2 * ROWS, :] = values[...]
    count = jnp.broadcast_to(jnp.sum(even, keepdims=True), (16, HEAD_DIM))
    packed[2 * ROWS :, :] = count.astype(jnp.bfloat16)


def pack(keys, values, logprob, docs, response):
    wide = (ROWS // 128, 128)
    return pl.pallas_call(
        pack_kernel,
        out_shape=(
            pltpu.VMEM((PACKED, HEAD_DIM), jnp.bfloat16),
            jax.ShapeDtypeStruct((ROWS, HEAD_DIM), jnp.float32),
        ),
        in_specs=[VMEM] * 5,
        out_specs=(VMEM,) * 2,
        cost_estimate=pl.CostEstimate(flops=10000, bytes_accessed=MIB // 2, transcendentals=0),
    )(keys, values, logprob.reshape(wide), docs.reshape(wide), response.reshape(wide))


def spans():
    return [(block, slice(block * ROWS, (block + 1) * ROWS)) for block in range(BLOCKS)]


def attend_kernel(
    queries, grads, own, near, far, opposite, own_s, near_s, far_s, opposite_s,
    attention, grad_queries, own_part, near_part, far_part, opposite_part, swap_parts,
    opposite_s_part,
    keys, values, keys_t, values_t, bias, scores, probs, grad_scores, acc_k, acc_v,
):
    place = lax.axis_index("ka")
    core = lax.rem(place, 2)
    chip = lax.rem(place // 2, CHIPS)
    step = 1 - 2 * core
    chips = [chip, chip - step, chip + step, chip + 2, chip, chip + step, chip - step, chip + 2]
    first_row = lax.rem(place, BLOCKS) * ROWS
    blocks = (own, near, far, opposite, own_s, near_s, far_s, opposite_s)
    parts = (
        own_part, near_part, far_part, opposite_part,
        swap_parts.at[0], swap_parts.at[1], swap_parts.at[2], opposite_s_part,
    )
    count = None
    for block, span in spans():
        key = blocks[block][:ROWS, :]
        value = blocks[block][ROWS : 2 * ROWS, :]
        keys[span, :] = key
        values[span, :] = value
        keys_t[:, span] = key.T
        values_t[:, span] = value.T
        term = blocks[block][2 * ROWS :, :].astype(jnp.float32)
        count = term if count is None else count + term
    cut = count[:1, :1].astype(jnp.int32)
    row = first_row + lax.broadcasted_iota(jnp.int32, (ROWS, ROWS), 0)
    lane = lax.broadcasted_iota(jnp.int32, (ROWS, ROWS), 1)
    start = jnp.where(row >= cut, cut, 0)
    for block, span in spans():
        side = core if block < CHIPS else 1 - core
        col = lane + (lax.rem(chips[block] + CHIPS, CHIPS) * 2 + side) * ROWS
        bias[:, span] = jnp.where((col >= start) & (col <= row), 0.0, NEG)

    columns = [slice(head * HEAD_DIM, (head + 1) * HEAD_DIM) for head in range(HEADS)]

    def score_step(head, span, top):
        score = dot(queries[:, columns[head]], keys_t[:, span]) + bias[:, span]
        scores[head % 2, :, span] = score
        folded = jnp.maximum(score[:, :128], score[:, 128:])
        return folded if top is None else jnp.maximum(top, folded)

    def prob_step(head, span, row_max, total):
        prob = jnp.exp2(scores[head % 2, :, span] * SCALE2 - row_max)
        probs[head % 2, :, span] = prob.astype(jnp.bfloat16)
        folded = prob[:, :128] + prob[:, 128:]
        return folded if total is None else total + folded

    def max_of(top):
        return jnp.max(top, axis=1, keepdims=True) * SCALE2

    top = total = None
    for block, span in spans():
        top = score_step(0, span, top)
    row_max = max_of(top)
    for block, span in spans():
        total = prob_step(0, span, row_max, total)
    for head in range(HEADS):
        slot = head % 2
        query = queries[:, columns[head]]
        inv_total = 1.0 / jnp.sum(total, axis=1, keepdims=True)
        output = (dot(probs[slot], values[...]) * inv_total).astype(jnp.bfloat16)
        attention[:, columns[head]] = output
        grad_wide = grads[:, columns[head]].astype(jnp.float32)
        delta = jnp.sum(grad_wide * output.astype(jnp.float32), axis=1, keepdims=True) * inv_total
        grad_scaled = (grad_wide * inv_total).astype(jnp.bfloat16)
        top = total = None
        for block, span in spans():
            grad_prob = dot(grad_scaled, values_t[:, span])
            if head < HEADS - 1:
                top = score_step(head + 1, span, top)
            grad_score = probs[slot, :, span].astype(jnp.float32) * (grad_prob - delta)
            grad_scores[slot, :, span] = grad_score.astype(jnp.bfloat16)
        if head < HEADS - 1:
            row_max = max_of(top)
        query_t = query.T
        grad_t = grad_scaled.T
        for block, span in spans():
            part_k = dot(query_t, grad_scores[slot, :, span])
            part_v = dot(grad_t, probs[slot, :, span])
            if head < HEADS - 1:
                total = prob_step(head + 1, span, row_max, total)
            if head:
                part_k += acc_k[:, span]
                part_v += acc_v[:, span]
            if head < HEADS - 1:
                acc_k[:, span] = part_k
                acc_v[:, span] = part_v
            else:
                parts[block][:, :HEAD_DIM] = (part_k * INV_ROOT).astype(jnp.bfloat16).T
                parts[block][:, HEAD_DIM:] = part_v.astype(jnp.bfloat16).T
        grad_queries[:, columns[head]] = dot(grad_scores[slot], keys[...]) * INV_ROOT


def attend(queries, grads, blocks):
    width = HEADS * HEAD_DIM
    part = jax.ShapeDtypeStruct((ROWS, 2 * HEAD_DIM), jnp.bfloat16)
    return pl.pallas_call(
        attend_kernel,
        out_shape=(
            jax.ShapeDtypeStruct((ROWS, width), jnp.bfloat16),
            jax.ShapeDtypeStruct((ROWS, width), jnp.float32),
            part,
            part,
            part,
            part,
            jax.ShapeDtypeStruct((3, ROWS, 2 * HEAD_DIM), jnp.bfloat16),
            part,
        ),
        in_specs=[VMEM] * (2 + BLOCKS),
        out_specs=(VMEM,) * 8,
        scratch_shapes=[
            pltpu.VMEM((PAIR_SPAN, HEAD_DIM), jnp.bfloat16),
            pltpu.VMEM((PAIR_SPAN, HEAD_DIM), jnp.bfloat16),
            pltpu.VMEM((HEAD_DIM, PAIR_SPAN), jnp.bfloat16),
            pltpu.VMEM((HEAD_DIM, PAIR_SPAN), jnp.bfloat16),
            pltpu.VMEM((ROWS, PAIR_SPAN), jnp.float32),
            pltpu.VMEM((2, ROWS, PAIR_SPAN), jnp.float32),
            pltpu.VMEM((2, ROWS, PAIR_SPAN), jnp.bfloat16),
            pltpu.VMEM((2, ROWS, PAIR_SPAN), jnp.bfloat16),
            pltpu.VMEM((HEAD_DIM, PAIR_SPAN), jnp.float32),
            pltpu.VMEM((HEAD_DIM, PAIR_SPAN), jnp.float32),
        ],
        compiler_params=pltpu.CompilerParams(vmem_limit_bytes=32 * MIB),
        cost_estimate=pl.CostEstimate(
            flops=12 * HEADS * ROWS * PAIR_SPAN * HEAD_DIM,
            bytes_accessed=4 * MIB,
            transcendentals=HEADS * ROWS * PAIR_SPAN,
        ),
    )(queries, grads, *blocks)


def at(half, chip, core):
    return half * 8 + (chip % CHIPS) * 2 + core


def per_device(queries, key_heads, value_heads, grad_output, token_logprob, doc_ids, response):
    spots = [(half, chip, core) for half in (0, 1) for chip in range(CHIPS) for core in (0, 1)]
    ahead = [(at(h, x, k), at(h, x + 1 - 2 * k, k)) for h, x, k in spots]
    cross = [(at(h, x, k), at(h, x + 1 - 2 * k, 1 - k)) for h, x, k in spots]
    back = [(there, here) for here, there in ahead]
    cross_back = [(there, here) for here, there in cross]
    swap = [(place, place ^ 1) for place in range(16)]

    def send(block, route):
        return lax.ppermute(block, "ka", route)

    def exchange(table, axis, masks):
        extent = range(lax.axis_size(axis))
        routes = [[(place, place ^ mask) for place in extent] for mask in masks]
        return sum((lax.ppermute(table, axis, route) for route in routes), table)

    own, sums = pack(key_heads, value_heads, token_logprob, doc_ids, response)
    queries, grad_output = fetch(queries, grad_output)
    columns = [list(range(low, 16, 2)) for low in (0, 1)]
    sums = lax.all_gather(sums, "pb", axis_index_groups=columns)
    sums = lax.optimization_barrier(sums)
    near = send(own, ahead)
    far = send(own, back)
    own_s = send(own, swap)
    opposite = send(near, ahead)
    opposite_s = send(near, cross)
    near_s = send(near, swap)
    far_s = send(far, swap)

    blocks = (own, near, far, opposite, own_s, near_s, far_s, opposite_s)
    attention, grad_queries, own_p, near_p, far_p, opposite_p, swap_p, opposite_s_p = attend(
        queries, grad_output, blocks
    )
    passed = send(opposite_p, back)
    passed_s = send(opposite_s_p, cross_back)
    swapped = send(swap_p, swap)
    wide = jnp.float32
    near_sum = (near_p.astype(wide) + swapped[1] + passed + passed_s).astype(jnp.bfloat16)
    far_sum = far_p + swapped[2]
    near_part = send(near_sum, back)
    far_part = send(far_sum, ahead)
    _, sums = lax.optimization_barrier((near_sum, sums))
    table = exchange(jnp.sum(sums[:, :8, :], axis=0), "ka", (1,))
    table = exchange(table, "ka", (2, 4, 6))
    table = exchange(table, ("pb", "ka"), (8, 16, 24))
    table = table[0].reshape(4, PAIRS)
    margins = table[0] / table[2] - table[1] / table[3]
    total = own_p.astype(wide) + swapped[0] + near_part + far_part
    return (attention, grad_queries, total[:, :HEAD_DIM], total[:, HEAD_DIM:], margins)


def solution(mesh):
    rows = P(("pb", "ka"), None)
    line = P(("pb", "ka"))
    return jax.shard_map(
        per_device,
        mesh=mesh,
        in_specs=(rows, rows, rows, rows, line, line, line),
        out_specs=(rows, rows, rows, rows, P()),
        check_vma=False,
    )
```

```python
import math

import jax
import jax.numpy as jnp
from jax import lax
from jax.experimental import pallas as pl
from jax.experimental.pallas import tpu as pltpu
from jax.sharding import PartitionSpec as P

HEAD_DIM = 128
HEADS = 6
PAIR_SPAN = 2048
ROWS = 256
BLOCKS = PAIR_SPAN // ROWS
CHIPS = 4
PAIRS = 32
PACKED = 2 * ROWS + 16
NEG = -1e30
INV_ROOT = 1.0 / math.sqrt(HEAD_DIM)
SCALE2 = INV_ROOT * math.log2(math.e)

VMEM = pl.BlockSpec(memory_space=pltpu.VMEM)
HBM = pl.BlockSpec(memory_space=pltpu.HBM)
MIB = 1024 * 1024


def dot(a, b):
    return jnp.dot(a, b, preferred_element_type=jnp.float32)


def fetch_kernel(queries_hbm, grads_hbm, queries, grads, arrived):
    fetches = [
        pltpu.make_async_copy(source, target, arrived.at[number])
        for number, (source, target) in enumerate(((queries_hbm, queries), (grads_hbm, grads)))
    ]
    for fetch in fetches:
        fetch.start()
    for fetch in fetches:
        fetch.wait()


def fetch(queries, grads):
    return pl.pallas_call(
        fetch_kernel,
        out_shape=(
            pltpu.VMEM(queries.shape, jnp.bfloat16),
            pltpu.VMEM(grads.shape, jnp.bfloat16),
        ),
        in_specs=[HBM] * 2,
        out_specs=(VMEM,) * 2,
        scratch_shapes=[pltpu.SemaphoreType.DMA((2,))],
        cost_estimate=pl.CostEstimate(flops=0, bytes_accessed=2 * MIB, transcendentals=0),
    )(*(pltpu.with_memory_space_constraint(x, pltpu.HBM) for x in (queries, grads)))


def split(value):
    high = value.astype(jnp.bfloat16).astype(jnp.float32)
    middle = (value - high).astype(jnp.bfloat16).astype(jnp.float32)
    return high, middle, value - high - middle


def pack_kernel(keys, values, logprob, docs, response, packed):
    odd = (docs[...] & 1).astype(jnp.float32)
    even = 1.0 - odd
    live = response[...].astype(jnp.float32)
    scored = logprob[...] * live
    first, second, first_live, second_live, count = (
        jnp.sum(term, keepdims=True)
        for term in (scored * even, scored * odd, live * even, live * odd, even)
    )
    terms = (*split(first), *split(second), first_live, second_live, count)
    lane = lax.broadcasted_iota(jnp.int32, (16, HEAD_DIM), 1)
    table = jnp.zeros((16, HEAD_DIM), jnp.float32)
    for place, term in enumerate(terms):
        table = jnp.where(lane == place, term, table)
    packed[:ROWS, :] = keys[...]
    packed[ROWS : 2 * ROWS, :] = values[...]
    packed[2 * ROWS :, :] = table.astype(jnp.bfloat16)


def pack(keys, values, logprob, docs, response):
    wide = (ROWS // 128, 128)
    return pl.pallas_call(
        pack_kernel,
        out_shape=pltpu.VMEM((PACKED, HEAD_DIM), jnp.bfloat16),
        in_specs=[VMEM] * 5,
        out_specs=VMEM,
        cost_estimate=pl.CostEstimate(flops=10000, bytes_accessed=MIB // 2, transcendentals=0),
    )(keys, values, logprob.reshape(wide), docs.reshape(wide), response.reshape(wide))


def spans():
    return [(block, slice(block * ROWS, (block + 1) * ROWS)) for block in range(BLOCKS)]


def attend_kernel(
    queries, grads, own, near, far, opposite, own_s, near_s, far_s, opposite_s,
    attention, grad_queries, own_part, near_part, far_part, opposite_part, swap_parts,
    opposite_s_part, margin,
    keys, values, keys_t, values_t, bias, scores, probs, grad_scores, acc_k, acc_v,
):
    place = lax.axis_index("ka")
    core = lax.rem(place, 2)
    chip = lax.rem(place // 2, CHIPS)
    step = 1 - 2 * core
    chips = [chip, chip - step, chip + step, chip + 2, chip, chip + step, chip - step, chip + 2]
    first_row = lax.rem(place, BLOCKS) * ROWS
    blocks = (own, near, far, opposite, own_s, near_s, far_s, opposite_s)
    parts = (
        own_part, near_part, far_part, opposite_part,
        swap_parts.at[0], swap_parts.at[1], swap_parts.at[2], opposite_s_part,
    )
    totals = None
    for block, span in spans():
        key = blocks[block][:ROWS, :]
        value = blocks[block][ROWS : 2 * ROWS, :]
        keys[span, :] = key
        values[span, :] = value
        keys_t[:, span] = key.T
        values_t[:, span] = value.T
        term = blocks[block][2 * ROWS :, :].astype(jnp.float32)
        totals = term if totals is None else totals + term
    totals = totals[:8, :]
    wide = lax.broadcasted_iota(jnp.int32, (8, HEAD_DIM), 1)

    def total_of(low, high):
        chosen = jnp.where((wide >= low) & (wide < high), totals, 0.0)
        return jnp.sum(chosen, axis=1, keepdims=True)

    pair = lax.axis_index("pb") * 2 + place // BLOCKS
    value = total_of(0, 3) / total_of(6, 7) - total_of(3, 6) / total_of(7, 8)
    margin[...] = jnp.where(wide == pair, value, 0.0)
    cut = total_of(8, 9)[:1].astype(jnp.int32)
    row = first_row + lax.broadcasted_iota(jnp.int32, (ROWS, ROWS), 0)
    lane = lax.broadcasted_iota(jnp.int32, (ROWS, ROWS), 1)
    start = jnp.where(row >= cut, cut, 0)
    for block, span in spans():
        side = core if block < CHIPS else 1 - core
        col = lane + (lax.rem(chips[block] + CHIPS, CHIPS) * 2 + side) * ROWS
        bias[:, span] = jnp.where((col >= start) & (col <= row), 0.0, NEG)

    columns = [slice(head * HEAD_DIM, (head + 1) * HEAD_DIM) for head in range(HEADS)]

    def score_step(head, span, top):
        score = dot(queries[:, columns[head]], keys_t[:, span]) + bias[:, span]
        scores[head % 2, :, span] = score
        folded = jnp.maximum(score[:, :128], score[:, 128:])
        return folded if top is None else jnp.maximum(top, folded)

    def prob_step(head, span, row_max, total):
        prob = jnp.exp2(scores[head % 2, :, span] * SCALE2 - row_max)
        probs[head % 2, :, span] = prob.astype(jnp.bfloat16)
        folded = prob[:, :128] + prob[:, 128:]
        return folded if total is None else total + folded

    def max_of(top):
        return jnp.max(top, axis=1, keepdims=True) * SCALE2

    top = total = None
    for block, span in spans():
        top = score_step(0, span, top)
    row_max = max_of(top)
    for block, span in spans():
        total = prob_step(0, span, row_max, total)
    for head in range(HEADS):
        slot = head % 2
        query = queries[:, columns[head]]
        inv_total = 1.0 / jnp.sum(total, axis=1, keepdims=True)
        output = (dot(probs[slot], values[...]) * inv_total).astype(jnp.bfloat16)
        attention[:, columns[head]] = output
        grad_wide = grads[:, columns[head]].astype(jnp.float32)
        delta = jnp.sum(grad_wide * output.astype(jnp.float32), axis=1, keepdims=True) * inv_total
        grad_scaled = (grad_wide * inv_total).astype(jnp.bfloat16)
        top = total = None
        for block, span in spans():
            grad_prob = dot(grad_scaled, values_t[:, span])
            if head < HEADS - 1:
                top = score_step(head + 1, span, top)
            grad_score = probs[slot, :, span].astype(jnp.float32) * (grad_prob - delta)
            grad_scores[slot, :, span] = grad_score.astype(jnp.bfloat16)
        if head < HEADS - 1:
            row_max = max_of(top)
        query_t = query.T
        grad_t = grad_scaled.T
        for block, span in spans():
            part_k = dot(query_t, grad_scores[slot, :, span])
            part_v = dot(grad_t, probs[slot, :, span])
            if head < HEADS - 1:
                total = prob_step(head + 1, span, row_max, total)
            if head:
                part_k += acc_k[:, span]
                part_v += acc_v[:, span]
            if head < HEADS - 1:
                acc_k[:, span] = part_k
                acc_v[:, span] = part_v
            else:
                parts[block][:, :HEAD_DIM] = (part_k * INV_ROOT).astype(jnp.bfloat16).T
                parts[block][:, HEAD_DIM:] = part_v.astype(jnp.bfloat16).T
        grad_queries[:, columns[head]] = dot(grad_scores[slot], keys[...]) * INV_ROOT


def attend(queries, grads, blocks):
    width = HEADS * HEAD_DIM
    part = jax.ShapeDtypeStruct((ROWS, 2 * HEAD_DIM), jnp.bfloat16)
    return pl.pallas_call(
        attend_kernel,
        out_shape=(
            jax.ShapeDtypeStruct((ROWS, width), jnp.bfloat16),
            jax.ShapeDtypeStruct((ROWS, width), jnp.float32),
            part,
            part,
            part,
            part,
            jax.ShapeDtypeStruct((3, ROWS, 2 * HEAD_DIM), jnp.bfloat16),
            part,
            jax.ShapeDtypeStruct((8, HEAD_DIM), jnp.float32),
        ),
        in_specs=[VMEM] * (2 + BLOCKS),
        out_specs=(VMEM,) * 9,
        scratch_shapes=[
            pltpu.VMEM((PAIR_SPAN, HEAD_DIM), jnp.bfloat16),
            pltpu.VMEM((PAIR_SPAN, HEAD_DIM), jnp.bfloat16),
            pltpu.VMEM((HEAD_DIM, PAIR_SPAN), jnp.bfloat16),
            pltpu.VMEM((HEAD_DIM, PAIR_SPAN), jnp.bfloat16),
            pltpu.VMEM((ROWS, PAIR_SPAN), jnp.float32),
            pltpu.VMEM((2, ROWS, PAIR_SPAN), jnp.float32),
            pltpu.VMEM((2, ROWS, PAIR_SPAN), jnp.bfloat16),
            pltpu.VMEM((2, ROWS, PAIR_SPAN), jnp.bfloat16),
            pltpu.VMEM((HEAD_DIM, PAIR_SPAN), jnp.float32),
            pltpu.VMEM((HEAD_DIM, PAIR_SPAN), jnp.float32),
        ],
        compiler_params=pltpu.CompilerParams(vmem_limit_bytes=32 * MIB),
        cost_estimate=pl.CostEstimate(
            flops=12 * HEADS * ROWS * PAIR_SPAN * HEAD_DIM,
            bytes_accessed=4 * MIB,
            transcendentals=HEADS * ROWS * PAIR_SPAN,
        ),
    )(queries, grads, *blocks)


def at(half, chip, core):
    return half * 8 + (chip % CHIPS) * 2 + core


def per_device(queries, key_heads, value_heads, grad_output, token_logprob, doc_ids, response):
    spots = [(half, chip, core) for half in (0, 1) for chip in range(CHIPS) for core in (0, 1)]
    ahead = [(at(h, x, k), at(h, x + 1 - 2 * k, k)) for h, x, k in spots]
    cross = [(at(h, x, k), at(h, x + 1 - 2 * k, 1 - k)) for h, x, k in spots]
    back = [(there, here) for here, there in ahead]
    cross_back = [(there, here) for here, there in cross]
    swap = [(place, place ^ 1) for place in range(16)]

    def send(block, route):
        return lax.ppermute(block, "ka", route)

    def exchange(table, axis, mask):
        route = [(place, place ^ mask) for place in range(16)]
        return table + lax.ppermute(table, axis, route)

    own = pack(key_heads, value_heads, token_logprob, doc_ids, response)
    queries, grad_output = fetch(queries, grad_output)
    near = send(own, ahead)
    far = send(own, back)
    own_s = send(own, swap)
    opposite = send(near, ahead)
    opposite_s = send(near, cross)
    near_s = send(near, swap)
    far_s = send(far, swap)

    blocks = (own, near, far, opposite, own_s, near_s, far_s, opposite_s)
    attention, grad_queries, own_p, near_p, far_p, opposite_p, swap_p, opposite_s_p, margin = (
        attend(queries, grad_output, blocks)
    )
    swapped = send(swap_p, swap)
    passed = send(opposite_p, back)
    passed_s = send(opposite_s_p, cross_back)
    margin = exchange(margin, "pb", 8)
    swapped, margin = lax.optimization_barrier((swapped, margin))
    margin = exchange(margin, "pb", 4)
    passed, margin = lax.optimization_barrier((passed, margin))
    wide = jnp.float32
    near_sum = (near_p.astype(wide) + swapped[1] + passed + passed_s).astype(jnp.bfloat16)
    far_sum = far_p + swapped[2]
    near_part = send(near_sum, back)
    far_part = send(far_sum, ahead)
    margin = exchange(margin, "pb", 2)
    far_part, margin = lax.optimization_barrier((far_part, margin))
    margin = exchange(margin, "pb", 1)
    margin = exchange(margin, "ka", 8)
    total = own_p.astype(wide) + swapped[0] + near_part + far_part
    return (
        attention, grad_queries, total[:, :HEAD_DIM], total[:, HEAD_DIM:], margin[0, :PAIRS]
    )


def solution(mesh):
    rows = P(("pb", "ka"), None)
    line = P(("pb", "ka"))
    return jax.shard_map(
        per_device,
        mesh=mesh,
        in_specs=(rows, rows, rows, rows, line, line, line),
        out_specs=(rows, rows, rows, rows, P()),
        check_vma=False,
    )
```

```python
import math

import jax
import jax.numpy as jnp
from jax import lax
from jax.experimental import pallas as pl
from jax.experimental.pallas import tpu as pltpu
from jax.sharding import PartitionSpec as P

HEAD_DIM = 128
HEADS = 6
PAIR_SPAN = 2048
ROWS = 256
BLOCKS = PAIR_SPAN // ROWS
CHIPS = 4
PAIRS = 32
PACKED = 2 * ROWS + 16
NEG = -1e30
INV_ROOT = 1.0 / math.sqrt(HEAD_DIM)
SCALE2 = INV_ROOT * math.log2(math.e)

VMEM = pl.BlockSpec(memory_space=pltpu.VMEM)
HBM = pl.BlockSpec(memory_space=pltpu.HBM)
MIB = 1024 * 1024


def dot(a, b):
    return jnp.dot(a, b, preferred_element_type=jnp.float32)


def fetch_kernel(queries_hbm, grads_hbm, queries, grads, arrived):
    fetches = [
        pltpu.make_async_copy(source, target, arrived.at[number])
        for number, (source, target) in enumerate(((queries_hbm, queries), (grads_hbm, grads)))
    ]
    for fetch in fetches:
        fetch.start()
    for fetch in fetches:
        fetch.wait()


def fetch(queries, grads):
    return pl.pallas_call(
        fetch_kernel,
        out_shape=(
            pltpu.VMEM(queries.shape, jnp.bfloat16),
            pltpu.VMEM(grads.shape, jnp.bfloat16),
        ),
        in_specs=[HBM] * 2,
        out_specs=(VMEM,) * 2,
        scratch_shapes=[pltpu.SemaphoreType.DMA((2,))],
        cost_estimate=pl.CostEstimate(flops=0, bytes_accessed=2 * MIB, transcendentals=0),
    )(*(pltpu.with_memory_space_constraint(x, pltpu.HBM) for x in (queries, grads)))


def split(value):
    high = value.astype(jnp.bfloat16).astype(jnp.float32)
    middle = (value - high).astype(jnp.bfloat16).astype(jnp.float32)
    return high, middle, value - high - middle


def pack_kernel(keys, values, logprob, docs, response, packed):
    odd = (docs[...] & 1).astype(jnp.float32)
    even = 1.0 - odd
    live = response[...].astype(jnp.float32)
    scored = logprob[...] * live
    first, second, first_live, second_live, count = (
        jnp.sum(term, keepdims=True)
        for term in (scored * even, scored * odd, live * even, live * odd, even)
    )
    terms = (*split(first), *split(second), first_live, second_live, count)
    lane = lax.broadcasted_iota(jnp.int32, (16, HEAD_DIM), 1)
    table = jnp.zeros((16, HEAD_DIM), jnp.float32)
    for place, term in enumerate(terms):
        table = jnp.where(lane == place, term, table)
    packed[:ROWS, :] = keys[...]
    packed[ROWS : 2 * ROWS, :] = values[...]
    packed[2 * ROWS :, :] = table.astype(jnp.bfloat16)


def pack(keys, values, logprob, docs, response):
    wide = (ROWS // 128, 128)
    return pl.pallas_call(
        pack_kernel,
        out_shape=pltpu.VMEM((PACKED, HEAD_DIM), jnp.bfloat16),
        in_specs=[VMEM] * 5,
        out_specs=VMEM,
        cost_estimate=pl.CostEstimate(flops=10000, bytes_accessed=MIB // 2, transcendentals=0),
    )(keys, values, logprob.reshape(wide), docs.reshape(wide), response.reshape(wide))


def total_of(totals, low, high):
    lane = lax.broadcasted_iota(jnp.int32, totals.shape, 1)
    chosen = jnp.where((lane >= low) & (lane < high), totals, 0.0)
    return jnp.sum(chosen, axis=1, keepdims=True)


def margin_kernel(*refs):
    totals = refs[0][2 * ROWS :, :].astype(jnp.float32)
    for ref in refs[1:BLOCKS]:
        totals += ref[2 * ROWS :, :].astype(jnp.float32)
    totals = totals[:8, :]
    pair = lax.axis_index("pb") * 2 + lax.axis_index("ka") // BLOCKS
    first = total_of(totals, 0, 3) / total_of(totals, 6, 7)
    second = total_of(totals, 3, 6) / total_of(totals, 7, 8)
    lane = lax.broadcasted_iota(jnp.int32, (8, HEAD_DIM), 1)
    refs[BLOCKS][...] = jnp.where(lane == pair, first - second, 0.0)


def pair_margin(blocks):
    return pl.pallas_call(
        margin_kernel,
        out_shape=pltpu.VMEM((8, HEAD_DIM), jnp.float32),
        in_specs=[VMEM] * BLOCKS,
        out_specs=VMEM,
        cost_estimate=pl.CostEstimate(flops=10000, bytes_accessed=65536, transcendentals=0),
    )(*blocks)


def spans():
    return [(block, slice(block * ROWS, (block + 1) * ROWS)) for block in range(BLOCKS)]


def attend_kernel(
    queries, grads, own, near, far, opposite, own_s, near_s, far_s, opposite_s,
    attention, grad_queries, own_part, near_part, far_part, opposite_part, swap_parts,
    opposite_s_part,
    keys, values, keys_t, values_t, bias, scores, probs, grad_scores, acc_k, acc_v,
):
    place = lax.axis_index("ka")
    core = lax.rem(place, 2)
    chip = lax.rem(place // 2, CHIPS)
    step = 1 - 2 * core
    chips = [chip, chip - step, chip + step, chip + 2, chip, chip + step, chip - step, chip + 2]
    first_row = lax.rem(place, BLOCKS) * ROWS
    blocks = (own, near, far, opposite, own_s, near_s, far_s, opposite_s)
    parts = (
        own_part, near_part, far_part, opposite_part,
        swap_parts.at[0], swap_parts.at[1], swap_parts.at[2], opposite_s_part,
    )
    totals = None
    for block, span in spans():
        key = blocks[block][:ROWS, :]
        value = blocks[block][ROWS : 2 * ROWS, :]
        keys[span, :] = key
        values[span, :] = value
        keys_t[:, span] = key.T
        values_t[:, span] = value.T
        term = blocks[block][2 * ROWS :, :].astype(jnp.float32)
        totals = term if totals is None else totals + term
    totals = totals[:8, :]
    cut = total_of(totals, 8, 9)[:1].astype(jnp.int32)
    row = first_row + lax.broadcasted_iota(jnp.int32, (ROWS, ROWS), 0)
    lane = lax.broadcasted_iota(jnp.int32, (ROWS, ROWS), 1)
    start = jnp.where(row >= cut, cut, 0)
    for block, span in spans():
        side = core if block < CHIPS else 1 - core
        col = lane + (lax.rem(chips[block] + CHIPS, CHIPS) * 2 + side) * ROWS
        bias[:, span] = jnp.where((col >= start) & (col <= row), 0.0, NEG)

    columns = [slice(head * HEAD_DIM, (head + 1) * HEAD_DIM) for head in range(HEADS)]

    def score_step(head, span, top):
        score = dot(queries[:, columns[head]], keys_t[:, span]) + bias[:, span]
        scores[head % 2, :, span] = score
        folded = jnp.maximum(score[:, :128], score[:, 128:])
        return folded if top is None else jnp.maximum(top, folded)

    def prob_step(head, span, row_max, total):
        prob = jnp.exp2(scores[head % 2, :, span] * SCALE2 - row_max)
        probs[head % 2, :, span] = prob.astype(jnp.bfloat16)
        folded = prob[:, :128] + prob[:, 128:]
        return folded if total is None else total + folded

    def max_of(top):
        return jnp.max(top, axis=1, keepdims=True) * SCALE2

    top = total = None
    for block, span in spans():
        top = score_step(0, span, top)
    row_max = max_of(top)
    for block, span in spans():
        total = prob_step(0, span, row_max, total)
    for head in range(HEADS):
        slot = head % 2
        query = queries[:, columns[head]]
        inv_total = 1.0 / jnp.sum(total, axis=1, keepdims=True)
        output = (dot(probs[slot], values[...]) * inv_total).astype(jnp.bfloat16)
        attention[:, columns[head]] = output
        grad_wide = grads[:, columns[head]].astype(jnp.float32)
        delta = jnp.sum(grad_wide * output.astype(jnp.float32), axis=1, keepdims=True) * inv_total
        grad_scaled = (grad_wide * inv_total).astype(jnp.bfloat16)
        top = total = None
        for block, span in spans():
            grad_prob = dot(grad_scaled, values_t[:, span])
            if head < HEADS - 1:
                top = score_step(head + 1, span, top)
            grad_score = probs[slot, :, span].astype(jnp.float32) * (grad_prob - delta)
            grad_scores[slot, :, span] = grad_score.astype(jnp.bfloat16)
        if head < HEADS - 1:
            row_max = max_of(top)
        query_t = query.T
        grad_t = grad_scaled.T
        for block, span in spans():
            part_k = dot(query_t, grad_scores[slot, :, span])
            part_v = dot(grad_t, probs[slot, :, span])
            if head < HEADS - 1:
                total = prob_step(head + 1, span, row_max, total)
            if head:
                part_k += acc_k[:, span]
                part_v += acc_v[:, span]
            if head < HEADS - 1:
                acc_k[:, span] = part_k
                acc_v[:, span] = part_v
            else:
                parts[block][:, :HEAD_DIM] = (part_k * INV_ROOT).astype(jnp.bfloat16).T
                parts[block][:, HEAD_DIM:] = part_v.astype(jnp.bfloat16).T
        grad_queries[:, columns[head]] = dot(grad_scores[slot], keys[...]) * INV_ROOT


def attend(queries, grads, blocks):
    width = HEADS * HEAD_DIM
    part = jax.ShapeDtypeStruct((ROWS, 2 * HEAD_DIM), jnp.bfloat16)
    return pl.pallas_call(
        attend_kernel,
        out_shape=(
            jax.ShapeDtypeStruct((ROWS, width), jnp.bfloat16),
            jax.ShapeDtypeStruct((ROWS, width), jnp.float32),
            part,
            part,
            part,
            part,
            jax.ShapeDtypeStruct((3, ROWS, 2 * HEAD_DIM), jnp.bfloat16),
            part,
        ),
        in_specs=[VMEM] * (2 + BLOCKS),
        out_specs=(VMEM,) * 8,
        scratch_shapes=[
            pltpu.VMEM((PAIR_SPAN, HEAD_DIM), jnp.bfloat16),
            pltpu.VMEM((PAIR_SPAN, HEAD_DIM), jnp.bfloat16),
            pltpu.VMEM((HEAD_DIM, PAIR_SPAN), jnp.bfloat16),
            pltpu.VMEM((HEAD_DIM, PAIR_SPAN), jnp.bfloat16),
            pltpu.VMEM((ROWS, PAIR_SPAN), jnp.float32),
            pltpu.VMEM((2, ROWS, PAIR_SPAN), jnp.float32),
            pltpu.VMEM((2, ROWS, PAIR_SPAN), jnp.bfloat16),
            pltpu.VMEM((2, ROWS, PAIR_SPAN), jnp.bfloat16),
            pltpu.VMEM((HEAD_DIM, PAIR_SPAN), jnp.float32),
            pltpu.VMEM((HEAD_DIM, PAIR_SPAN), jnp.float32),
        ],
        compiler_params=pltpu.CompilerParams(vmem_limit_bytes=32 * MIB),
        cost_estimate=pl.CostEstimate(
            flops=12 * HEADS * ROWS * PAIR_SPAN * HEAD_DIM,
            bytes_accessed=4 * MIB,
            transcendentals=HEADS * ROWS * PAIR_SPAN,
        ),
    )(queries, grads, *blocks)


def at(half, chip, core):
    return half * 8 + (chip % CHIPS) * 2 + core


def per_device(queries, key_heads, value_heads, grad_output, token_logprob, doc_ids, response):
    spots = [(half, chip, core) for half in (0, 1) for chip in range(CHIPS) for core in (0, 1)]
    ahead = [(at(h, x, k), at(h, x + 1 - 2 * k, k)) for h, x, k in spots]
    cross = [(at(h, x, k), at(h, x + 1 - 2 * k, 1 - k)) for h, x, k in spots]
    back = [(there, here) for here, there in ahead]
    cross_back = [(there, here) for here, there in cross]
    swap = [(place, place ^ 1) for place in range(16)]

    def send(block, route):
        return lax.ppermute(block, "ka", route)

    def exchange(table, axis, *masks):
        routes = [[(place, place ^ mask) for place in range(16)] for mask in masks]
        return sum((lax.ppermute(table, axis, route) for route in routes), table)

    own = pack(key_heads, value_heads, token_logprob, doc_ids, response)
    queries, grad_output = fetch(queries, grad_output)
    near = send(own, ahead)
    own_s = send(own, swap)
    own_later, own_s = lax.optimization_barrier((own, own_s))
    far = send(own_later, back)
    opposite = send(near, ahead)
    opposite_s = send(near, cross)
    near_s = send(near, swap)
    far_s = send(far, swap)

    blocks = (own, near, far, opposite, own_s, near_s, far_s, opposite_s)
    margin = pair_margin(blocks)
    near, margin = lax.optimization_barrier((near, margin))
    blocks = (own, near, far, opposite, own_s, near_s, far_s, opposite_s)
    margin = exchange(margin, "pb", 4, 8, 12)
    attention, grad_queries, own_p, near_p, far_p, opposite_p, swap_p, opposite_s_p = attend(
        queries, grad_output, blocks
    )
    own_p, near_p, far_p, opposite_p, swap_p, opposite_s_p, margin = lax.optimization_barrier(
        (own_p, near_p, far_p, opposite_p, swap_p, opposite_s_p, margin)
    )
    swapped = send(swap_p, swap)
    passed = send(opposite_p, back)
    passed_s = send(opposite_s_p, cross_back)
    margin = exchange(margin, "pb", 2)
    swapped, margin = lax.optimization_barrier((swapped, margin))
    margin = exchange(margin, "pb", 1)
    passed, passed_s, margin = lax.optimization_barrier((passed, passed_s, margin))
    wide = jnp.float32
    near_sum = (near_p.astype(wide) + swapped[1] + passed + passed_s).astype(jnp.bfloat16)
    far_sum = far_p + swapped[2]
    near_part = send(near_sum, back)
    far_part = send(far_sum, ahead)
    margin = exchange(margin, "ka", 8)
    total = own_p.astype(wide) + swapped[0] + near_part + far_part
    return (
        attention, grad_queries, total[:, :HEAD_DIM], total[:, HEAD_DIM:], margin[0, :PAIRS]
    )


def solution(mesh):
    rows = P(("pb", "ka"), None)
    line = P(("pb", "ka"))
    return jax.shard_map(
        per_device,
        mesh=mesh,
        in_specs=(rows, rows, rows, rows, line, line, line),
        out_specs=(rows, rows, rows, rows, P()),
        check_vma=False,
    )
```

```python
import math

import jax
import jax.numpy as jnp
from jax import lax
from jax.experimental import pallas as pl
from jax.experimental.pallas import tpu as pltpu
from jax.sharding import PartitionSpec as P

HEAD_DIM = 128
HEADS = 6
PAIR_SPAN = 2048
ROWS = 256
BLOCKS = PAIR_SPAN // ROWS
CHIPS = 4
PAIRS = 32
PACKED = 2 * ROWS + 16
NEG = -1e30
INV_ROOT = 1.0 / math.sqrt(HEAD_DIM)
SCALE2 = INV_ROOT * math.log2(math.e)

VMEM = pl.BlockSpec(memory_space=pltpu.VMEM)
HBM = pl.BlockSpec(memory_space=pltpu.HBM)
MIB = 1024 * 1024


def dot(a, b):
    return jnp.dot(a, b, preferred_element_type=jnp.float32)


def fetch_kernel(queries_hbm, grads_hbm, queries, grads, arrived):
    fetches = [
        pltpu.make_async_copy(source, target, arrived.at[number])
        for number, (source, target) in enumerate(((queries_hbm, queries), (grads_hbm, grads)))
    ]
    for fetch in fetches:
        fetch.start()
    for fetch in fetches:
        fetch.wait()


def fetch(queries, grads):
    return pl.pallas_call(
        fetch_kernel,
        out_shape=(
            pltpu.VMEM(queries.shape, jnp.bfloat16),
            pltpu.VMEM(grads.shape, jnp.bfloat16),
        ),
        in_specs=[HBM] * 2,
        out_specs=(VMEM,) * 2,
        scratch_shapes=[pltpu.SemaphoreType.DMA((2,))],
        cost_estimate=pl.CostEstimate(flops=0, bytes_accessed=2 * MIB, transcendentals=0),
    )(*(pltpu.with_memory_space_constraint(x, pltpu.HBM) for x in (queries, grads)))


def split(value):
    high = value.astype(jnp.bfloat16).astype(jnp.float32)
    middle = (value - high).astype(jnp.bfloat16).astype(jnp.float32)
    return high, middle, value - high - middle


def pack_kernel(keys, values, logprob, docs, response, packed):
    odd = (docs[...] & 1).astype(jnp.float32)
    even = 1.0 - odd
    live = response[...].astype(jnp.float32)
    scored = logprob[...] * live
    first, second, first_live, second_live, count = (
        jnp.sum(term, keepdims=True)
        for term in (scored * even, scored * odd, live * even, live * odd, even)
    )
    terms = (*split(first), *split(second), first_live, second_live, count)
    lane = lax.broadcasted_iota(jnp.int32, (16, HEAD_DIM), 1)
    table = jnp.zeros((16, HEAD_DIM), jnp.float32)
    for place, term in enumerate(terms):
        table = jnp.where(lane == place, term, table)
    packed[:ROWS, :] = keys[...]
    packed[ROWS : 2 * ROWS, :] = values[...]
    packed[2 * ROWS :, :] = table.astype(jnp.bfloat16)


def pack(keys, values, logprob, docs, response):
    wide = (ROWS // 128, 128)
    return pl.pallas_call(
        pack_kernel,
        out_shape=pltpu.VMEM((PACKED, HEAD_DIM), jnp.bfloat16),
        in_specs=[VMEM] * 5,
        out_specs=VMEM,
        cost_estimate=pl.CostEstimate(flops=10000, bytes_accessed=MIB // 2, transcendentals=0),
    )(keys, values, logprob.reshape(wide), docs.reshape(wide), response.reshape(wide))


def total_of(totals, low, high):
    lane = lax.broadcasted_iota(jnp.int32, totals.shape, 1)
    chosen = jnp.where((lane >= low) & (lane < high), totals, 0.0)
    return jnp.sum(chosen, axis=1, keepdims=True)


def margin_kernel(*refs):
    totals = refs[0][2 * ROWS :, :].astype(jnp.float32)
    for ref in refs[1:BLOCKS]:
        totals += ref[2 * ROWS :, :].astype(jnp.float32)
    totals = totals[:8, :]
    pair = lax.axis_index("pb") * 2 + lax.axis_index("ka") // BLOCKS
    first = total_of(totals, 0, 3) / total_of(totals, 6, 7)
    second = total_of(totals, 3, 6) / total_of(totals, 7, 8)
    lane = lax.broadcasted_iota(jnp.int32, (8, HEAD_DIM), 1)
    refs[BLOCKS][...] = jnp.where(lane == pair, first - second, 0.0)


def pair_margin(blocks):
    return pl.pallas_call(
        margin_kernel,
        out_shape=pltpu.VMEM((8, HEAD_DIM), jnp.float32),
        in_specs=[VMEM] * BLOCKS,
        out_specs=VMEM,
        compiler_params=pltpu.CompilerParams(vmem_limit_bytes=MIB),
        cost_estimate=pl.CostEstimate(flops=10000, bytes_accessed=65536, transcendentals=0),
    )(*blocks)


def spans():
    return [(block, slice(block * ROWS, (block + 1) * ROWS)) for block in range(BLOCKS)]


def attend_kernel(
    queries, grads, own, near, far, opposite, own_s, near_s, far_s, opposite_s,
    attention, grad_queries, own_part, near_part, far_part, opposite_part, swap_parts,
    opposite_s_part,
    keys, values, keys_t, values_t, bias, scores, probs, grad_scores, acc_k, acc_v,
):
    place = lax.axis_index("ka")
    core = lax.rem(place, 2)
    chip = lax.rem(place // 2, CHIPS)
    step = 1 - 2 * core
    chips = [chip, chip - step, chip + step, chip + 2, chip, chip + step, chip - step, chip + 2]
    first_row = lax.rem(place, BLOCKS) * ROWS
    blocks = (own, near, far, opposite, own_s, near_s, far_s, opposite_s)
    parts = (
        own_part, near_part, far_part, opposite_part,
        swap_parts.at[0], swap_parts.at[1], swap_parts.at[2], opposite_s_part,
    )
    totals = None
    for block, span in spans():
        key = blocks[block][:ROWS, :]
        value = blocks[block][ROWS : 2 * ROWS, :]
        keys[span, :] = key
        values[span, :] = value
        keys_t[:, span] = key.T
        values_t[:, span] = value.T
        term = blocks[block][2 * ROWS :, :].astype(jnp.float32)
        totals = term if totals is None else totals + term
    totals = totals[:8, :]
    cut = total_of(totals, 8, 9)[:1].astype(jnp.int32)
    row = first_row + lax.broadcasted_iota(jnp.int32, (ROWS, ROWS), 0)
    lane = lax.broadcasted_iota(jnp.int32, (ROWS, ROWS), 1)
    start = jnp.where(row >= cut, cut, 0)
    for block, span in spans():
        side = core if block < CHIPS else 1 - core
        col = lane + (lax.rem(chips[block] + CHIPS, CHIPS) * 2 + side) * ROWS
        bias[:, span] = jnp.where((col >= start) & (col <= row), 0.0, NEG)

    columns = [slice(head * HEAD_DIM, (head + 1) * HEAD_DIM) for head in range(HEADS)]

    def score_step(head, span, top):
        score = dot(queries[:, columns[head]], keys_t[:, span]) + bias[:, span]
        scores[head % 2, :, span] = score
        folded = jnp.maximum(score[:, :128], score[:, 128:])
        return folded if top is None else jnp.maximum(top, folded)

    def prob_step(head, span, row_max, total):
        prob = jnp.exp2(scores[head % 2, :, span] * SCALE2 - row_max)
        probs[head % 2, :, span] = prob.astype(jnp.bfloat16)
        folded = prob[:, :128] + prob[:, 128:]
        return folded if total is None else total + folded

    def max_of(top):
        return jnp.max(top, axis=1, keepdims=True) * SCALE2

    top = total = None
    for block, span in spans():
        top = score_step(0, span, top)
    row_max = max_of(top)
    for block, span in spans():
        total = prob_step(0, span, row_max, total)
    for head in range(HEADS):
        slot = head % 2
        query = queries[:, columns[head]]
        inv_total = 1.0 / jnp.sum(total, axis=1, keepdims=True)
        output = (dot(probs[slot], values[...]) * inv_total).astype(jnp.bfloat16)
        attention[:, columns[head]] = output
        grad_wide = grads[:, columns[head]].astype(jnp.float32)
        delta = jnp.sum(grad_wide * output.astype(jnp.float32), axis=1, keepdims=True) * inv_total
        grad_scaled = (grad_wide * inv_total).astype(jnp.bfloat16)
        top = total = None
        for block, span in spans():
            grad_prob = dot(grad_scaled, values_t[:, span])
            if head < HEADS - 1:
                top = score_step(head + 1, span, top)
            grad_score = probs[slot, :, span].astype(jnp.float32) * (grad_prob - delta)
            grad_scores[slot, :, span] = grad_score.astype(jnp.bfloat16)
        if head < HEADS - 1:
            row_max = max_of(top)
        query_t = query.T
        grad_t = grad_scaled.T
        for block, span in spans():
            part_k = dot(query_t, grad_scores[slot, :, span])
            part_v = dot(grad_t, probs[slot, :, span])
            if head < HEADS - 1:
                total = prob_step(head + 1, span, row_max, total)
            if head:
                part_k += acc_k[:, span]
                part_v += acc_v[:, span]
            if head < HEADS - 1:
                acc_k[:, span] = part_k
                acc_v[:, span] = part_v
            else:
                parts[block][:, :HEAD_DIM] = (part_k * INV_ROOT).astype(jnp.bfloat16).T
                parts[block][:, HEAD_DIM:] = part_v.astype(jnp.bfloat16).T
        grad_queries[:, columns[head]] = dot(grad_scores[slot], keys[...]) * INV_ROOT


def attend(queries, grads, blocks):
    width = HEADS * HEAD_DIM
    part = jax.ShapeDtypeStruct((ROWS, 2 * HEAD_DIM), jnp.bfloat16)
    return pl.pallas_call(
        attend_kernel,
        out_shape=(
            jax.ShapeDtypeStruct((ROWS, width), jnp.bfloat16),
            jax.ShapeDtypeStruct((ROWS, width), jnp.float32),
            part,
            part,
            part,
            part,
            jax.ShapeDtypeStruct((3, ROWS, 2 * HEAD_DIM), jnp.bfloat16),
            part,
        ),
        in_specs=[VMEM] * (2 + BLOCKS),
        out_specs=(VMEM,) * 8,
        scratch_shapes=[
            pltpu.VMEM((PAIR_SPAN, HEAD_DIM), jnp.bfloat16),
            pltpu.VMEM((PAIR_SPAN, HEAD_DIM), jnp.bfloat16),
            pltpu.VMEM((HEAD_DIM, PAIR_SPAN), jnp.bfloat16),
            pltpu.VMEM((HEAD_DIM, PAIR_SPAN), jnp.bfloat16),
            pltpu.VMEM((ROWS, PAIR_SPAN), jnp.float32),
            pltpu.VMEM((2, ROWS, PAIR_SPAN), jnp.float32),
            pltpu.VMEM((2, ROWS, PAIR_SPAN), jnp.bfloat16),
            pltpu.VMEM((2, ROWS, PAIR_SPAN), jnp.bfloat16),
            pltpu.VMEM((HEAD_DIM, PAIR_SPAN), jnp.float32),
            pltpu.VMEM((HEAD_DIM, PAIR_SPAN), jnp.float32),
        ],
        compiler_params=pltpu.CompilerParams(vmem_limit_bytes=32 * MIB),
        cost_estimate=pl.CostEstimate(
            flops=12 * HEADS * ROWS * PAIR_SPAN * HEAD_DIM,
            bytes_accessed=4 * MIB,
            transcendentals=HEADS * ROWS * PAIR_SPAN,
        ),
    )(queries, grads, *blocks)


def at(half, chip, core):
    return half * 8 + (chip % CHIPS) * 2 + core


def per_device(queries, key_heads, value_heads, grad_output, token_logprob, doc_ids, response):
    spots = [(half, chip, core) for half in (0, 1) for chip in range(CHIPS) for core in (0, 1)]
    ahead = [(at(h, x, k), at(h, x + 1 - 2 * k, k)) for h, x, k in spots]
    cross = [(at(h, x, k), at(h, x + 1 - 2 * k, 1 - k)) for h, x, k in spots]
    back = [(there, here) for here, there in ahead]
    cross_back = [(there, here) for here, there in cross]
    swap = [(place, place ^ 1) for place in range(16)]

    def send(block, route):
        return lax.ppermute(block, "ka", route)

    def exchange(table, axis, *masks):
        extent = range(lax.axis_size(axis))
        routes = [[(place, place ^ mask) for place in extent] for mask in masks]
        return sum((lax.ppermute(table, axis, route) for route in routes), table)

    own = pack(key_heads, value_heads, token_logprob, doc_ids, response)
    queries, grad_output = fetch(queries, grad_output)
    near = send(own, ahead)
    own_s = send(own, swap)
    own_later, own_s = lax.optimization_barrier((own, own_s))
    far = send(own_later, back)
    opposite = send(near, ahead)
    opposite_s = send(near, cross)
    near_s = send(near, swap)
    far_s = send(far, swap)

    blocks = (own, near, far, opposite, own_s, near_s, far_s, opposite_s)
    margin = pair_margin(blocks)
    near, margin = lax.optimization_barrier((near, margin))
    blocks = (own, near, far, opposite, own_s, near_s, far_s, opposite_s)
    margin = exchange(margin, "pb", 8)
    attention, grad_queries, own_p, near_p, far_p, opposite_p, swap_p, opposite_s_p = attend(
        queries, grad_output, blocks
    )
    own_p, near_p, far_p, opposite_p, swap_p, opposite_s_p, margin = lax.optimization_barrier(
        (own_p, near_p, far_p, opposite_p, swap_p, opposite_s_p, margin)
    )
    swapped = send(swap_p, swap)
    passed = send(opposite_p, back)
    passed_s = send(opposite_s_p, cross_back)
    margin = exchange(margin, "pb", 4)
    swapped, margin = lax.optimization_barrier((swapped, margin))
    margin = exchange(margin, "pb", 2)
    passed, passed_s, margin = lax.optimization_barrier((passed, passed_s, margin))
    wide = jnp.float32
    near_sum = (near_p.astype(wide) + swapped[1] + passed + passed_s).astype(jnp.bfloat16)
    far_sum = far_p + swapped[2]
    near_part = send(near_sum, back)
    far_part = send(far_sum, ahead)
    margin = exchange(margin, "pb", 1)
    far_part, margin = lax.optimization_barrier((far_part, margin))
    margin = exchange(margin, "ka", 8)
    total = own_p.astype(wide) + swapped[0] + near_part + far_part
    return (
        attention, grad_queries, total[:, :HEAD_DIM], total[:, HEAD_DIM:], margin[0, :PAIRS]
    )


def solution(mesh):
    rows = P(("pb", "ka"), None)
    line = P(("pb", "ka"))
    return jax.shard_map(
        per_device,
        mesh=mesh,
        in_specs=(rows, rows, rows, rows, line, line, line),
        out_specs=(rows, rows, rows, rows, P()),
        check_vma=False,
    )
```

```python
import math

import jax
import jax.numpy as jnp
from jax import lax
from jax.experimental import pallas as pl
from jax.experimental.pallas import tpu as pltpu
from jax.sharding import PartitionSpec as P

HEAD_DIM = 128
HEADS = 6
PAIR_SPAN = 2048
ROWS = 256
BLOCKS = PAIR_SPAN // ROWS
CHIPS = 4
PAIRS = 32
PACKED = 2 * ROWS + 16
NEG = -1e30
INV_ROOT = 1.0 / math.sqrt(HEAD_DIM)
SCALE2 = INV_ROOT * math.log2(math.e)

VMEM = pl.BlockSpec(memory_space=pltpu.VMEM)
HBM = pl.BlockSpec(memory_space=pltpu.HBM)
MIB = 1024 * 1024


def dot(a, b):
    return jnp.dot(a, b, preferred_element_type=jnp.float32)


def fetch_kernel(queries_hbm, grads_hbm, queries, grads, arrived):
    fetches = [
        pltpu.make_async_copy(source, target, arrived.at[number])
        for number, (source, target) in enumerate(((queries_hbm, queries), (grads_hbm, grads)))
    ]
    for fetch in fetches:
        fetch.start()
    for fetch in fetches:
        fetch.wait()


def fetch(queries, grads):
    return pl.pallas_call(
        fetch_kernel,
        out_shape=(
            pltpu.VMEM(queries.shape, jnp.bfloat16),
            pltpu.VMEM(grads.shape, jnp.bfloat16),
        ),
        in_specs=[HBM] * 2,
        out_specs=(VMEM,) * 2,
        scratch_shapes=[pltpu.SemaphoreType.DMA((2,))],
        cost_estimate=pl.CostEstimate(flops=0, bytes_accessed=2 * MIB, transcendentals=0),
    )(*(pltpu.with_memory_space_constraint(x, pltpu.HBM) for x in (queries, grads)))


def split(value):
    high = value.astype(jnp.bfloat16).astype(jnp.float32)
    middle = (value - high).astype(jnp.bfloat16).astype(jnp.float32)
    return high, middle, value - high - middle


def pack_kernel(keys, values, logprob, docs, response, packed):
    odd = (docs[...] & 1).astype(jnp.float32)
    even = 1.0 - odd
    live = response[...].astype(jnp.float32)
    scored = logprob[...] * live
    first, second, first_live, second_live, count = (
        jnp.sum(term, keepdims=True)
        for term in (scored * even, scored * odd, live * even, live * odd, even)
    )
    terms = (*split(first), *split(second), first_live, second_live, count)
    lane = lax.broadcasted_iota(jnp.int32, (16, HEAD_DIM), 1)
    table = jnp.zeros((16, HEAD_DIM), jnp.float32)
    for place, term in enumerate(terms):
        table = jnp.where(lane == place, term, table)
    packed[:ROWS, :] = keys[...]
    packed[ROWS : 2 * ROWS, :] = values[...]
    packed[2 * ROWS :, :] = table.astype(jnp.bfloat16)


def pack(keys, values, logprob, docs, response):
    wide = (ROWS // 128, 128)
    return pl.pallas_call(
        pack_kernel,
        out_shape=pltpu.VMEM((PACKED, HEAD_DIM), jnp.bfloat16),
        in_specs=[VMEM] * 5,
        out_specs=VMEM,
        cost_estimate=pl.CostEstimate(flops=10000, bytes_accessed=MIB // 2, transcendentals=0),
    )(keys, values, logprob.reshape(wide), docs.reshape(wide), response.reshape(wide))


def total_of(totals, low, high):
    lane = lax.broadcasted_iota(jnp.int32, totals.shape, 1)
    chosen = jnp.where((lane >= low) & (lane < high), totals, 0.0)
    return jnp.sum(chosen, axis=1, keepdims=True)


def margin_kernel(*refs):
    totals = refs[0][2 * ROWS :, :].astype(jnp.float32)
    for ref in refs[1:BLOCKS]:
        totals += ref[2 * ROWS :, :].astype(jnp.float32)
    totals = totals[:8, :]
    pair = lax.axis_index("pb") * 2 + lax.axis_index("ka") // BLOCKS
    first = total_of(totals, 0, 3) / total_of(totals, 6, 7)
    second = total_of(totals, 3, 6) / total_of(totals, 7, 8)
    lane = lax.broadcasted_iota(jnp.int32, (8, HEAD_DIM), 1)
    refs[BLOCKS][...] = jnp.where(lane == pair, first - second, 0.0)


def pair_margin(blocks):
    return pl.pallas_call(
        margin_kernel,
        out_shape=pltpu.VMEM((8, HEAD_DIM), jnp.float32),
        in_specs=[VMEM] * BLOCKS,
        out_specs=VMEM,
        compiler_params=pltpu.CompilerParams(vmem_limit_bytes=MIB),
        cost_estimate=pl.CostEstimate(flops=10000, bytes_accessed=65536, transcendentals=0),
    )(*blocks)


def spans():
    return [(block, slice(block * ROWS, (block + 1) * ROWS)) for block in range(BLOCKS)]


def attend_kernel(
    queries, grads, own, near, far, opposite, own_s, near_s, far_s, opposite_s,
    attention, grad_queries, own_part, near_part, far_part, opposite_part, swap_parts,
    opposite_s_part,
    keys, values, keys_t, values_t, bias, scores, probs, grad_scores, acc_k, acc_v,
):
    place = lax.axis_index("ka")
    core = lax.rem(place, 2)
    chip = lax.rem(place // 2, CHIPS)
    step = 1 - 2 * core
    chips = [chip, chip - step, chip + step, chip + 2, chip, chip + step, chip - step, chip + 2]
    first_row = lax.rem(place, BLOCKS) * ROWS
    blocks = (own, near, far, opposite, own_s, near_s, far_s, opposite_s)
    parts = (
        own_part, near_part, far_part, opposite_part,
        swap_parts.at[0], swap_parts.at[1], swap_parts.at[2], opposite_s_part,
    )
    totals = None
    for block, span in spans():
        key = blocks[block][:ROWS, :]
        value = blocks[block][ROWS : 2 * ROWS, :]
        keys[span, :] = key
        values[span, :] = value
        keys_t[:, span] = key.T
        values_t[:, span] = value.T
        term = blocks[block][2 * ROWS :, :].astype(jnp.float32)
        totals = term if totals is None else totals + term
    totals = totals[:8, :]
    cut = total_of(totals, 8, 9)[:1].astype(jnp.int32)
    row = first_row + lax.broadcasted_iota(jnp.int32, (ROWS, ROWS), 0)
    lane = lax.broadcasted_iota(jnp.int32, (ROWS, ROWS), 1)
    start = jnp.where(row >= cut, cut, 0)
    for block, span in spans():
        side = core if block < CHIPS else 1 - core
        col = lane + (lax.rem(chips[block] + CHIPS, CHIPS) * 2 + side) * ROWS
        bias[:, span] = jnp.where((col >= start) & (col <= row), 0.0, NEG)

    columns = [slice(head * HEAD_DIM, (head + 1) * HEAD_DIM) for head in range(HEADS)]

    def score_step(head, span, top):
        score = dot(queries[:, columns[head]], keys_t[:, span]) + bias[:, span]
        scores[head % 2, :, span] = score
        folded = jnp.maximum(score[:, :128], score[:, 128:])
        return folded if top is None else jnp.maximum(top, folded)

    def prob_step(head, span, row_max, total):
        prob = jnp.exp2(scores[head % 2, :, span] * SCALE2 - row_max)
        probs[head % 2, :, span] = prob.astype(jnp.bfloat16)
        folded = prob[:, :128] + prob[:, 128:]
        return folded if total is None else total + folded

    def max_of(top):
        return jnp.max(top, axis=1, keepdims=True) * SCALE2

    top = total = None
    for block, span in spans():
        top = score_step(0, span, top)
    row_max = max_of(top)
    for block, span in spans():
        total = prob_step(0, span, row_max, total)
    for head in range(HEADS):
        slot = head % 2
        query = queries[:, columns[head]]
        inv_total = 1.0 / jnp.sum(total, axis=1, keepdims=True)
        output = (dot(probs[slot], values[...]) * inv_total).astype(jnp.bfloat16)
        attention[:, columns[head]] = output
        grad_wide = grads[:, columns[head]].astype(jnp.float32)
        delta = jnp.sum(grad_wide * output.astype(jnp.float32), axis=1, keepdims=True) * inv_total
        grad_scaled = (grad_wide * inv_total).astype(jnp.bfloat16)
        top = total = None
        for block, span in spans():
            grad_prob = dot(grad_scaled, values_t[:, span])
            if head < HEADS - 1:
                top = score_step(head + 1, span, top)
            grad_score = probs[slot, :, span].astype(jnp.float32) * (grad_prob - delta)
            grad_scores[slot, :, span] = grad_score.astype(jnp.bfloat16)
        if head < HEADS - 1:
            row_max = max_of(top)
        query_t = query.T
        grad_t = grad_scaled.T
        for block, span in spans():
            part_k = dot(query_t, grad_scores[slot, :, span])
            part_v = dot(grad_t, probs[slot, :, span])
            if head < HEADS - 1:
                total = prob_step(head + 1, span, row_max, total)
            if head:
                part_k += acc_k[:, span]
                part_v += acc_v[:, span]
            if head < HEADS - 1:
                acc_k[:, span] = part_k
                acc_v[:, span] = part_v
            else:
                parts[block][:, :HEAD_DIM] = (part_k * INV_ROOT).astype(jnp.bfloat16).T
                parts[block][:, HEAD_DIM:] = part_v.astype(jnp.bfloat16).T
        grad_queries[:, columns[head]] = dot(grad_scores[slot], keys[...]) * INV_ROOT


def attend(queries, grads, blocks):
    width = HEADS * HEAD_DIM
    part = jax.ShapeDtypeStruct((ROWS, 2 * HEAD_DIM), jnp.bfloat16)
    return pl.pallas_call(
        attend_kernel,
        out_shape=(
            jax.ShapeDtypeStruct((ROWS, width), jnp.bfloat16),
            jax.ShapeDtypeStruct((ROWS, width), jnp.float32),
            part,
            part,
            part,
            part,
            jax.ShapeDtypeStruct((3, ROWS, 2 * HEAD_DIM), jnp.bfloat16),
            part,
        ),
        in_specs=[VMEM] * (2 + BLOCKS),
        out_specs=(VMEM,) * 8,
        scratch_shapes=[
            pltpu.VMEM((PAIR_SPAN, HEAD_DIM), jnp.bfloat16),
            pltpu.VMEM((PAIR_SPAN, HEAD_DIM), jnp.bfloat16),
            pltpu.VMEM((HEAD_DIM, PAIR_SPAN), jnp.bfloat16),
            pltpu.VMEM((HEAD_DIM, PAIR_SPAN), jnp.bfloat16),
            pltpu.VMEM((ROWS, PAIR_SPAN), jnp.float32),
            pltpu.VMEM((2, ROWS, PAIR_SPAN), jnp.float32),
            pltpu.VMEM((2, ROWS, PAIR_SPAN), jnp.bfloat16),
            pltpu.VMEM((2, ROWS, PAIR_SPAN), jnp.bfloat16),
            pltpu.VMEM((HEAD_DIM, PAIR_SPAN), jnp.float32),
            pltpu.VMEM((HEAD_DIM, PAIR_SPAN), jnp.float32),
        ],
        compiler_params=pltpu.CompilerParams(vmem_limit_bytes=32 * MIB),
        cost_estimate=pl.CostEstimate(
            flops=12 * HEADS * ROWS * PAIR_SPAN * HEAD_DIM,
            bytes_accessed=4 * MIB,
            transcendentals=HEADS * ROWS * PAIR_SPAN,
        ),
    )(queries, grads, *blocks)


def at(half, chip, core):
    return half * 8 + (chip % CHIPS) * 2 + core


def per_device(queries, key_heads, value_heads, grad_output, token_logprob, doc_ids, response):
    spots = [(half, chip, core) for half in (0, 1) for chip in range(CHIPS) for core in (0, 1)]
    ahead = [(at(h, x, k), at(h, x + 1 - 2 * k, k)) for h, x, k in spots]
    cross = [(at(h, x, k), at(h, x + 1 - 2 * k, 1 - k)) for h, x, k in spots]
    back = [(there, here) for here, there in ahead]
    cross_back = [(there, here) for here, there in cross]
    swap = [(place, place ^ 1) for place in range(16)]

    def send(block, route):
        return lax.ppermute(block, "ka", route)

    def exchange(table, axis, *masks):
        extent = range(lax.axis_size(axis))
        routes = [[(place, place ^ mask) for place in extent] for mask in masks]
        return sum((lax.ppermute(table, axis, route) for route in routes), table)

    own = pack(key_heads, value_heads, token_logprob, doc_ids, response)
    queries, grad_output = fetch(queries, grad_output)
    near = send(own, ahead)
    own_s = send(own, swap)
    own_later, own_s = lax.optimization_barrier((own, own_s))
    far = send(own_later, back)
    opposite = send(near, ahead)
    opposite_s = send(near, cross)
    near_later, far = lax.optimization_barrier((near, far))
    near_s = send(near_later, swap)
    far_s = send(far, swap)

    blocks = (own, near, far, opposite, own_s, near_s, far_s, opposite_s)
    margin = pair_margin(blocks)
    near, margin = lax.optimization_barrier((near, margin))
    blocks = (own, near, far, opposite, own_s, near_s, far_s, opposite_s)
    margin = exchange(margin, "pb", 8)
    attention, grad_queries, own_p, near_p, far_p, opposite_p, swap_p, opposite_s_p = attend(
        queries, grad_output, blocks
    )
    own_p, near_p, far_p, opposite_p, swap_p, opposite_s_p, margin = lax.optimization_barrier(
        (own_p, near_p, far_p, opposite_p, swap_p, opposite_s_p, margin)
    )
    swapped = send(swap_p, swap)
    passed = send(opposite_p, back)
    passed_s = send(opposite_s_p, cross_back)
    margin = exchange(margin, "pb", 4)
    swapped, margin = lax.optimization_barrier((swapped, margin))
    margin = exchange(margin, "pb", 2)
    passed, passed_s, margin = lax.optimization_barrier((passed, passed_s, margin))
    wide = jnp.float32
    near_sum = (near_p.astype(wide) + swapped[1] + passed + passed_s).astype(jnp.bfloat16)
    far_sum = far_p + swapped[2]
    near_part = send(near_sum, back)
    far_part = send(far_sum, ahead)
    _, far_part, margin = lax.optimization_barrier((near_sum, far_part, margin))
    margin = exchange(margin, ("pb", "ka"), 8, 16, 24)
    total = own_p.astype(wide) + swapped[0] + near_part + far_part
    return (
        attention, grad_queries, total[:, :HEAD_DIM], total[:, HEAD_DIM:], margin[0, :PAIRS]
    )


def solution(mesh):
    rows = P(("pb", "ka"), None)
    line = P(("pb", "ka"))
    return jax.shard_map(
        per_device,
        mesh=mesh,
        in_specs=(rows, rows, rows, rows, line, line, line),
        out_specs=(rows, rows, rows, rows, P()),
        check_vma=False,
    )
```
